128 devices in a mesh: expert: 8 (over z, core), chan: 16 (over x, y).
Axes of the slice: x: 4, y: 4, z: 4, core: 2. Of those that a mesh axis runs over, the one named last changes fastest.
Arguments:
- x_in: bfloat16 [1024, 16384], P(('expert', 'chan')), may hold values from -6 to 6
- z_in: bfloat16 [1024, 16384], P(('expert', 'chan')), may hold values from -6 to 6
- conv_state: bfloat16 [8, 3, 16384], P('expert', None, 'chan'), may hold values from -6 to 6
- ssm_state: float32 [8, 16, 16384], P('expert', None, 'chan'), may hold values from -6 to 6
- conv_weight: bfloat16 [4, 16384], P(None, 'chan'), may hold values from -3 to 3
- conv_bias: bfloat16 [16384], P('chan'), may hold values from -3 to 3
- proj_x: bfloat16 [16384, 544], P('chan'), may hold values from -0.046875 to 0.046875
- dt_gain: bfloat16 [512], replicated, may hold values from 0.5 to 1.5
- dt_weight: bfloat16 [512, 16384], P(None, 'chan'), may hold values from -0.25 to 0.25
- dt_bias: float32 [16384], P('chan'), may hold values from -5 to -1
- a_log: float32 [16, 16384], P(None, 'chan'), may hold values from 0 to 2.5
- skip_scale: float32 [16384], P('chan'), may hold values from 0.5 to 1.5
- out_weight: bfloat16 [16384, 8192], P('chan', 'expert'), may hold values from -0.046875 to 0.046875
- hidden: bfloat16 [1024, 8192], P(('expert', 'chan')), may hold values from -6 to 6
- moe_gain: bfloat16 [8192], replicated, may hold values from 0.5 to 1.5
- router: bfloat16 [8192, 4], replicated, may hold values from -0.125 to 0.125
- routes: int32 [1024, 2], P(('expert', 'chan')), may hold values from 0 to 3, all different within a row; in each aligned block of 8 rows (0 to 7, 8 to 15, ...) at most 5 rows name the same one
- gate_codes: bfloat16 [8, 8192, 6144], P('expert', None, 'chan'), may hold values from 0 to 15, as said below
- gate_zero: int32 [8, 64, 6144], P('expert', None, 'chan'), may hold values from 7 to 8
- gate_scale: bfloat16 [8, 64, 6144], P('expert', None, 'chan'), as said below
- up_codes: bfloat16 [8, 8192, 6144], P('expert', None, 'chan'), may hold values from 0 to 15, as said below
- up_zero: int32 [8, 64, 6144], P('expert', None, 'chan'), may hold values from 7 to 8
- up_scale: bfloat16 [8, 64, 6144], P('expert', None, 'chan'), as said below
- down_codes: bfloat16 [8, 6144, 8192], P('expert', 'chan'), may hold values from 0 to 15, as said below
- down_zero: int32 [8, 48, 8192], P('expert', 'chan'), may hold values from 7 to 8
- down_scale: bfloat16 [8, 48, 8192], P('expert', 'chan'), as said below
Outputs:
- layer_out: bfloat16 [1024, 8192], P(('expert', 'chan'))
- final_state: float32 [8, 16, 16384], P('expert', None, 'chan')
The draws below stay inside these ranges and needn't reach their ends.
Inputs may be any that keep to these rules, and one draw needn't show every extreme that they name: `routes`: in the rows of one device each expert is named by at most 5 rows, a bound that some block reaches. `gate_codes`: whole numbers. `up_codes`: whole numbers. `down_codes`: whole numbers. `gate_scale`: Positive. `up_scale`: Positive. `down_scale`: Positive.
All inputs are finite; a program needn't handle non-finite values.
Results may differ from the reference program's by a relative error of at most 0.04.
Values may be sent and summed in bfloat16 or wider, within the bound.
No kernel may reach another device: no remote copies, remote signals or barrier semaphores. Data moves between devices by JAX's collectives and lax.ppermute only.
A program may use at most 192 MiB of HBM per device.

```python
import math
import jax
import jax.numpy as jnp
import numpy as np
from jax import lax

D = 8192
INNER = 16384
STATE = 16
RANK = 512
KERNEL = 4
FF_WIN = 12288
GROUP = 128
TOK_DEV = 8
SEQS = 8
SEQ_LEN = 128
TOKENS = 1024
EXPERTS = 4
CAP = 5
N_EXPERT = 8
N_CHAN = 16


def code_table(key, shape):
    return jax.random.randint(key, shape, 0, 16).astype(jnp.float32).astype(jnp.bfloat16)


def scale_table(key, shape, fan_in):
    spread = jax.random.uniform(key, shape, jnp.float32, math.log(0.6), math.log(1.6))
    return (jnp.exp(spread) * (2.0 / (4.6 * math.sqrt(fan_in)))).astype(jnp.bfloat16)


def draw_gate_codes(key, part):
    key = jax.random.fold_in(key, 11)
    return code_table(key, (N_EXPERT, D, FF_WIN // 2))


def draw_up_codes(key, part):
    key = jax.random.fold_in(key, 12)
    return code_table(key, (N_EXPERT, D, FF_WIN // 2))


def draw_down_codes(key, part):
    key = jax.random.fold_in(key, 13)
    return code_table(key, (N_EXPERT, FF_WIN // 2, D))


def draw_gate_scale(key, part):
    key = jax.random.fold_in(key, 21)
    return scale_table(key, (N_EXPERT, D // GROUP, FF_WIN // 2), D)


def draw_up_scale(key, part):
    key = jax.random.fold_in(key, 22)
    return scale_table(key, (N_EXPERT, D // GROUP, FF_WIN // 2), D)


def draw_down_scale(key, part):
    key = jax.random.fold_in(key, 23)
    return scale_table(key, (N_EXPERT, FF_WIN // 2 // GROUP, D), FF_WIN)


def with_ends(result, key, least, largest):
    index_at = [jax.random.randint(jax.random.fold_in(key, axis), (), 0, length) for axis, length in enumerate(result.shape)]
    widest = result.shape.index(max(result.shape))
    next_to = index_at[:widest] + [(index_at[widest] + 1) % result.shape[widest]] + index_at[widest + 1:]
    return result.at[tuple(index_at)].set(least).at[tuple(next_to)].set(largest)


def block_levels(key, dims, pieces, smallest, top_value):
    def one(dim, shards_of):
        draws = jax.random.uniform(jax.random.fold_in(jax.random.fold_in(key, 6), dim), (shards_of,), jnp.float32, smallest / len(pieces), top_value / len(pieces))
        return jnp.repeat(jnp.exp(draws), dims[dim] // shards_of).reshape((-1,) + (1,) * (len(dims) - dim - 1))

    gain = one(*pieces[0])
    for cut in pieces[1:]:
        gain = gain * one(*cut)
    return gain


def shared_out(own_key, own, number, rows, count, top, bound, slope):
    ranking = jax.random.permutation(own_key, count)
    heavy_load, ordinary = load_shares(count, rows * top, bound, slope, True), load_shares(count, rows * top, bound, slope, False)
    places = jnp.arange(count)

    def named(sizes, rotation):
        used = int((sizes > 0).sum())
        fixed = max(1, used // 4)
        shifted = fixed + (places - fixed + rotation * (used - fixed)) % max(1, count - fixed)
        return jnp.zeros((count,), jnp.int32).at[ranking[jnp.where(places < fixed, places, shifted)]].set(jnp.asarray(sizes, jnp.int32))

    sizes = jnp.where(number % 4 == 0, named(heavy_load, number // 4), named(ordinary, number - number // 4 - 1))
    mixed = jax.random.permutation(jax.random.fold_in(own, 3), count)
    giver, taker = mixed[0:count // 2 * 2:2], mixed[1:count // 2 * 2:2]
    slack = jnp.minimum(sizes[giver] - 1, bound - sizes[taker]) // 2
    slack = jnp.where((giver == ranking[0]) | (taker == ranking[0]) | (sizes[taker] == 0), 0, jnp.maximum(slack, 0))
    shifted = jax.random.randint(jax.random.fold_in(own, 4), (count // 2,), 0, 1 << 20) % (slack + 1)
    sizes = sizes.at[giver].add(-shifted).at[taker].add(shifted)
    items = jnp.searchsorted(jnp.cumsum(sizes), jnp.arange(rows * top), side="right").astype(jnp.int32)
    table = items.reshape(top, rows).T
    table = table[jax.random.permutation(jax.random.fold_in(own, 1), rows)]
    rotation = jax.random.randint(jax.random.fold_in(own, 2), (rows, 1), 0, top)
    return jnp.take_along_axis(table, (jnp.arange(top)[None, :] + rotation) % top, axis=1)


def load_shares(count, total, most, skew, full):
    portions = [(1 << 20) // math.isqrt(standing ** skew) + 1 for standing in range(1, count + 1)]
    largest = most if full else min(most, max(-(-total // count), total * portions[0] // sum(portions)))
    least = 1 if total - largest >= count - 1 else 0
    given, rest = [largest] + [least] * (count - 1), total - largest - least * (count - 1)
    while rest > 0:
        candidates = [i for i in range(1, count) if given[i] < largest] or [i for i in range(1, count) if given[i] < most]
        pool, remaining = sum([portions[i] for i in candidates]), rest
        for i in candidates:
            more = min(most - given[i], max(1, remaining * portions[i] // pool), rest)
            given[i] = given[i] + more
            rest = rest - more
    return np.array(given)


def bell_draw(own_key, dims, scale, reach, split=(), held_as=jnp.bfloat16):
    gain = block_levels(own_key, dims, split, -0.22, 0.18) if split else 1.0
    entries = jax.random.normal(own_key, dims, jnp.float32) * scale * gain
    return jnp.minimum(jnp.maximum(entries, -reach), reach).astype(held_as)


def setup_inputs(seed: int = 0) -> dict:
    key_of = jax.random.split(jax.random.key(seed), 27)
    x_in = bell_draw(key_of[0], (TOKENS, INNER), 1.0, 6.0, ((0, 128),))
    z_in = bell_draw(key_of[1], (TOKENS, INNER), 1.0, 6.0, ((0, 128),))
    conv_state = bell_draw(key_of[2], (SEQS, KERNEL - 1, INNER), 1.0, 6.0, ((0, 8), (2, 16)))
    ssm_state = bell_draw(key_of[3], (SEQS, STATE, INNER), 1.0, 6.0, ((0, 8), (2, 16)), jnp.float32)
    conv_weight = bell_draw(key_of[4], (KERNEL, INNER), KERNEL ** -0.5, 3.0, ((1, 16),))
    conv_bias = bell_draw(key_of[5], (INNER,), 0.5, 3.0, ((0, 16),))
    proj_x = bell_draw(key_of[6], (INNER, RANK + 2 * STATE), INNER ** -0.5, 0.046875, ((0, 16),))
    dt_gain = jnp.clip(1.0 + 0.1 * jax.random.normal(key_of[7], (RANK,), jnp.float32), 0.5, 1.5).astype(jnp.bfloat16)
    dt_weight = bell_draw(key_of[8], (RANK, INNER), RANK ** -0.5, 0.25, ((1, 16),))
    dt_bias = jnp.clip(-5.0 + 4.0 * jax.random.uniform(key_of[9], (INNER,), jnp.float32) ** block_levels(key_of[9], (INNER,), ((0, 16),), -0.2, 0.2), -5.0, -1.0)
    a_log = jnp.clip(2.5 * jax.random.uniform(key_of[10], (STATE, INNER), jnp.float32) ** block_levels(key_of[10], (STATE, INNER), ((1, 16),), -0.2, 0.2), 0.0, 2.5)
    skip_scale = jnp.clip(0.5 + 1.0 * jax.random.uniform(key_of[11], (INNER,), jnp.float32) ** block_levels(key_of[11], (INNER,), ((0, 16),), -0.2, 0.2), 0.5, 1.5)
    out_weight = bell_draw(key_of[12], (INNER, D), INNER ** -0.5, 0.046875, ((0, 16), (1, 8)))
    hidden = bell_draw(key_of[13], (TOKENS, D), 1.0, 6.0, ((0, 128),))
    moe_gain = jnp.clip(1.0 + 0.1 * jax.random.normal(key_of[14], (D,), jnp.float32), 0.5, 1.5).astype(jnp.bfloat16)
    router = bell_draw(key_of[15], (D, EXPERTS), (D // 4) ** -0.5, 0.125)
    routes_keys = jax.random.split(jax.random.fold_in(key_of[16], 1), TOKENS // TOK_DEV)
    routes_turns = jax.random.permutation(jax.random.fold_in(key_of[16], 3), TOKENS // TOK_DEV)
    routes = jax.vmap(lambda own, number: shared_out(jax.random.fold_in(key_of[16], 2), own, number, TOK_DEV, EXPERTS, 2, CAP, 2))(routes_keys, routes_turns).reshape((TOKENS, 2))
    gate_codes = draw_gate_codes(jax.random.fold_in(key_of[26], 71), 0)
    gate_zero = with_ends(jax.random.randint(key_of[18], (N_EXPERT, D // GROUP, FF_WIN // 2), 7, 9), jax.random.fold_in(key_of[18], 1), 7, 8).astype(jnp.int32)
    gate_scale = draw_gate_scale(jax.random.fold_in(key_of[26], 71), 0)
    up_codes = draw_up_codes(jax.random.fold_in(key_of[26], 71), 0)
    up_zero = with_ends(jax.random.randint(key_of[21], (N_EXPERT, D // GROUP, FF_WIN // 2), 7, 9), jax.random.fold_in(key_of[21], 1), 7, 8).astype(jnp.int32)
    up_scale = draw_up_scale(jax.random.fold_in(key_of[26], 71), 0)
    down_codes = draw_down_codes(jax.random.fold_in(key_of[26], 71), 0)
    down_zero = with_ends(jax.random.randint(key_of[24], (N_EXPERT, FF_WIN // 2 // GROUP, D), 7, 9), jax.random.fold_in(key_of[24], 1), 7, 8).astype(jnp.int32)
    down_scale = draw_down_scale(jax.random.fold_in(key_of[26], 71), 0)
    return {"x_in": x_in, "z_in": z_in, "conv_state": conv_state, "ssm_state": ssm_state, "conv_weight": conv_weight, "conv_bias": conv_bias, "proj_x": proj_x, "dt_gain": dt_gain, "dt_weight": dt_weight, "dt_bias": dt_bias, "a_log": a_log, "skip_scale": skip_scale, "out_weight": out_weight, "hidden": hidden, "moe_gain": moe_gain, "router": router, "routes": routes, "gate_codes": gate_codes, "gate_zero": gate_zero, "gate_scale": gate_scale, "up_codes": up_codes, "up_zero": up_zero, "up_scale": up_scale, "down_codes": down_codes, "down_zero": down_zero, "down_scale": down_scale}


epsilon = 1e-05

def dequant(code_tab, zero_tab, scale_tab):
    groups = zero_tab.shape[0]
    shaped = code_tab.astype(jnp.float32).reshape(groups, code_tab.shape[0] // groups, code_tab.shape[1])
    dequant_vals = (shaped - zero_tab.astype(jnp.float32)[:, None, :]) * scale_tab.astype(jnp.float32)[:, None, :]
    return dequant_vals.reshape(code_tab.shape).astype(jnp.bfloat16)

def reference(x_in, z_in, conv_state, ssm_state, conv_weight, conv_bias, proj_x, dt_gain, dt_weight, dt_bias, a_log, skip_scale, out_weight, hidden, moe_gain, router, routes, gate_codes, gate_zero, gate_scale, up_codes, up_zero, up_scale, down_codes, down_zero, down_scale):
    x_seq = x_in.reshape(SEQS, SEQ_LEN, INNER)
    z_seq = z_in.reshape(SEQS, SEQ_LEN, INNER)
    extended = jnp.concatenate([conv_state, x_seq], axis=1).astype(jnp.float32)
    conv_pre = jnp.broadcast_to(conv_bias.astype(jnp.float32), x_seq.shape)
    for shift_pos in range(KERNEL):
        conv_pre = conv_pre + extended[:, shift_pos:shift_pos + SEQ_LEN] * conv_weight[shift_pos].astype(jnp.float32)
    u_act = jax.nn.silu(conv_pre).astype(jnp.bfloat16)
    u_float = u_act.astype(jnp.float32)
    projected = jnp.einsum('sle,ep->slp', u_float, proj_x.astype(jnp.float32))
    dt_low = projected[..., :RANK]
    b_mat = projected[..., RANK:RANK + STATE]
    c_mat = projected[..., RANK + STATE:]
    dt_norm = (dt_low * lax.rsqrt(lax.optimization_barrier(jnp.mean(dt_low * dt_low, axis=-1, keepdims=True)) + epsilon) * dt_gain.astype(jnp.float32)).astype(jnp.bfloat16)
    step_size = jax.nn.softplus(jnp.einsum('slr,re->sle', dt_norm.astype(jnp.float32), dt_weight.astype(jnp.float32)) + dt_bias)
    decay_rates = -jnp.exp(a_log)
    driven = step_size * u_float

    def advance(carried, inputs):
        d_row, du_row, b_row, c_row = inputs
        carried = jnp.exp(d_row[:, None, :] * decay_rates[None]) * carried + b_row[:, :, None] * du_row[:, None, :]
        return (carried, lax.optimization_barrier(jnp.sum(c_row[:, :, None] * carried, axis=1)))
    final_state, scanned = lax.scan(advance, ssm_state, (jnp.swapaxes(step_size, 0, 1), jnp.swapaxes(driven, 0, 1), jnp.swapaxes(b_mat, 0, 1), jnp.swapaxes(c_mat, 0, 1)))
    scan_out = jnp.swapaxes(scanned, 0, 1)
    y_out = ((scan_out + skip_scale * u_float) * jax.nn.silu(z_seq.astype(jnp.float32))).astype(jnp.bfloat16)
    mixer_out = jnp.dot(y_out.reshape(TOKENS, INNER), out_weight, preferred_element_type=jnp.float32)
    residual = hidden.astype(jnp.float32) + mixer_out
    normed = (residual * lax.rsqrt(lax.optimization_barrier(jnp.mean(residual * residual, axis=1, keepdims=True)) + epsilon) * moe_gain.astype(jnp.float32)).astype(jnp.bfloat16)
    logits = jnp.dot(normed, router, preferred_element_type=jnp.float32)
    weights = jnp.exp(logits)
    router_probs = weights / lax.optimization_barrier(jnp.sum(weights, axis=1, keepdims=True))
    route_gates = jnp.take_along_axis(router_probs, routes, axis=1)
    positions = jnp.arange(TOKENS, dtype=jnp.int32)
    most_rows = min(TOKENS, N_EXPERT * N_CHAN * CAP)
    lane_units = FF_WIN // (2 * N_CHAN)
    moe_out = jnp.zeros((TOKENS, D), jnp.float32)
    for expert_id in range(EXPERTS):
        routed = routes == expert_id
        routed_any = jnp.any(routed, axis=1)
        gate_k = lax.optimization_barrier(jnp.sum(jnp.where(routed, route_gates, 0.0), axis=1))
        ordering = jnp.argsort(jnp.where(routed_any, positions, positions + TOKENS), stable=True)[:most_rows].astype(jnp.int32)
        picked_rows = normed[ordering]
        expert_out = jnp.zeros((most_rows, D), jnp.float32)
        for half_id in range(2):
            weight_row = 2 * expert_id + half_id
            w_gate = dequant(gate_codes[weight_row], gate_zero[weight_row], gate_scale[weight_row])
            w_up = dequant(up_codes[weight_row], up_zero[weight_row], up_scale[weight_row])
            gate_pre = jnp.dot(picked_rows, w_gate, preferred_element_type=jnp.float32)
            up_pre = jnp.dot(picked_rows, w_up, preferred_element_type=jnp.float32)
            inner_act = (jax.nn.silu(gate_pre) * up_pre).astype(jnp.bfloat16)
            w_down = dequant(down_codes[weight_row], down_zero[weight_row], down_scale[weight_row])

            def add_lane(running, lane_id):
                lane_piece = lax.dynamic_slice_in_dim(inner_act, lane_id * lane_units, lane_units, 1)
                lane_down = lax.dynamic_slice_in_dim(w_down, lane_id * lane_units, lane_units, 0)
                lane_term = lax.optimization_barrier(jnp.dot(lane_piece, lane_down, preferred_element_type=jnp.float32).astype(jnp.bfloat16))
                return (running + lane_term.astype(jnp.float32), None)
            half_sum, unused = lax.scan(add_lane, jnp.zeros((most_rows, D), jnp.float32), jnp.arange(N_CHAN, dtype=jnp.int32))
            half_out = lax.optimization_barrier(half_sum.astype(jnp.bfloat16))
            expert_out = expert_out + half_out.astype(jnp.float32)
        contrib = jnp.where(routed_any[ordering][:, None], gate_k[ordering][:, None] * expert_out, 0.0)
        moe_out = moe_out.at[ordering].add(contrib)
    layer_out = (residual + moe_out).astype(jnp.bfloat16)
    return (layer_out, final_state)
```

```python
import jax
import jax.numpy as jnp
from jax import lax
from jax.experimental import pallas as pl
from jax.experimental.pallas import tpu as pltpu
from jax.sharding import Mesh, PartitionSpec as P

epsilon = 1e-05
f32 = jnp.float32
bf16 = jnp.bfloat16
RING = 4


def hop(value, axis, step):
    size = lax.axis_size(axis)
    return lax.ppermute(value, axis, [(i, (i + step) % size) for i in range(size)])


def pick(value, index, axis):
    return lax.dynamic_index_in_dim(value, index, axis, keepdims=False)


def spread(block, axis):
    behind, ahead = hop(block, axis, 1), hop(block, axis, -1)
    half = block.shape[-1] // 2
    across = jnp.concatenate(
        [hop(behind[..., :half], axis, 1), hop(ahead[..., half:], axis, -1)], axis=-1
    )
    return [block, behind, across, ahead]


def gather_sum(terms, axis, sign):
    total = terms[0].astype(f32)
    arrived = [hop(terms[s].astype(bf16), axis, sign * s) for s in (1, 2, 3)]
    for term in arrived:
        total = total + term.astype(f32)
    return total


def up_dequant_kernel(place, gc, gz, gs, uc, uz, us, gain, out):
    rows = gc.shape[0]
    groups = gz.shape[0]
    size = rows // groups
    width = gc.shape[1]
    half = groups // 2
    for codes, zero, scale, at in ((gc, gz, gs, 0), (uc, uz, us, width)):
        for g in range(groups):
            values = codes[pl.ds(g * size, size), :].astype(f32) - zero[pl.ds(g, 1), :].astype(f32)
            values = values * scale[pl.ds(g, 1), :]
            weight = gain[pl.ds(g * size, size), :]
            for lane in range(width // 128):
                out[g // half, 0, pl.ds((g % half) * size, size), pl.ds(at + lane * 128, 128)] = (
                    values[:, lane * 128 : (lane + 1) * 128] * weight
                ).astype(bf16)


def up_dequant(place, codes_a, zero_a, scale_a, codes_b, zero_b, scale_b, gain):
    model, width = codes_a.shape
    block = model // 8
    groups = zero_a.shape[0] // 8

    def source(dc, d, place):
        return (lax.rem(place[0] - d + RING, RING) * 2 + lax.rem(place[1] + dc, 2), 0)

    code_spec = pl.BlockSpec((block, width), source)
    group_spec = pl.BlockSpec((groups, width), source)
    return pl.pallas_call(
        up_dequant_kernel,
        grid_spec=pltpu.PrefetchScalarGridSpec(
            num_scalar_prefetch=1,
            grid=(2, RING),
            in_specs=[
                code_spec,
                group_spec,
                group_spec,
                code_spec,
                group_spec,
                group_spec,
                pl.BlockSpec((block, 128), source),
            ],
            out_specs=pl.BlockSpec(
                (2, 1, block // 2, 2 * width), lambda dc, d, place: (0, dc, d, 0)
            ),
        ),
        out_shape=jax.ShapeDtypeStruct((2, 2, model // 4, 2 * width), bf16),
        compiler_params=pltpu.CompilerParams(vmem_limit_bytes=32 * 1024 * 1024),
        cost_estimate=pl.CostEstimate(
            flops=8 * model * width, bytes_accessed=10 * model * width, transcendentals=0
        ),
        name="up_dequant",
    )(place, codes_a, zero_a, scale_a, codes_b, zero_b, scale_b, gain)


def down_dequant_kernel(place, codes, zero, scale, out):
    groups = zero.shape[0]
    size = codes.shape[0] // groups
    half = codes.shape[1] // 2
    for g in range(groups):
        rows = pl.ds(g * size, size)
        for part in range(2):
            cols = pl.ds(part * half, half)
            values = codes[rows, cols].astype(f32) - zero[pl.ds(g, 1), cols].astype(f32)
            out[0, part, rows, :] = (values * scale[pl.ds(g, 1), cols]).astype(bf16)


def down_dequant(place, codes, zero, scale):
    rows, model = codes.shape
    block = model // 8
    groups = zero.shape[0]

    def source(dc, d, place):
        return (0, d * 2 + lax.rem(place[1] + dc, 2))

    return pl.pallas_call(
        down_dequant_kernel,
        grid_spec=pltpu.PrefetchScalarGridSpec(
            num_scalar_prefetch=1,
            grid=(2, RING),
            in_specs=[
                pl.BlockSpec((rows, block), source),
                pl.BlockSpec((groups, block), source),
                pl.BlockSpec((groups, block), source),
            ],
            out_specs=pl.BlockSpec(
                (1, 2, rows, block // 2), lambda dc, d, place: (dc, 0, 0, d)
            ),
        ),
        out_shape=jax.ShapeDtypeStruct((2, 2, rows, model // 4), bf16),
        compiler_params=pltpu.CompilerParams(vmem_limit_bytes=32 * 1024 * 1024),
        cost_estimate=pl.CostEstimate(
            flops=3 * model * rows, bytes_accessed=4 * model * rows, transcendentals=0
        ),
        name="down_dequant",
    )(place, codes, zero, scale)


def pre_kernel(*refs, last, model):
    xs, rest = refs[:10], refs[10:]
    w = rest[0]
    if last:
        pre_in, sq_in, out, rows0, rows1, acc, sq = rest[1:]
    else:
        out, sq_out, rows0, rows1, acc, sq = rest[1:]
    k = pl.program_id(0)
    steps = pl.num_programs(0)
    group = xs[0].shape[0]

    @pl.when(k == 0)
    def _():
        acc[...] = jnp.zeros_like(acc)
        sq[...] = jnp.zeros_like(sq)

    for refs5, rows in ((xs[:5], rows0), (xs[5:], rows1)):
        rows[pl.ds(0, group), :] = refs5[0][...]
        rows[pl.ds(group, group), :] = refs5[1][...]

        @pl.when(k < steps // 2)
        def _(refs5=refs5, rows=rows):
            rows[pl.ds(2 * group, group), :] = refs5[3][...]

        @pl.when(k >= steps // 2)
        def _(refs5=refs5, rows=rows):
            rows[pl.ds(2 * group, group), :] = refs5[4][...]

        rows[pl.ds(3 * group, group), :] = refs5[2][...]
    width = acc.shape[1]
    tile = 256
    for n in range(width // tile):
        cols = pl.ds(n * tile, tile)
        acc[:, cols] += jnp.dot(
            rows0[...], w[0, 0, :, cols], preferred_element_type=f32
        ) + jnp.dot(rows1[...], w[0, 1, :, cols], preferred_element_type=f32)
    for r in range(4):
        at = pl.ds(r * group, group)
        total = sq[at, :]
        for rows in (rows0, rows1):
            for j in range(rows.shape[1] // 128):
                v = rows[at, pl.ds(j * 128, 128)].astype(f32)
                total = total + v * v
        sq[at, :] = total

    @pl.when(k == steps - 1)
    def _():
        if last:
            half = width // 2
            for r in range(4):
                at = pl.ds(r * group, group)
                square = jnp.sum(sq_in[at, :] + sq[at, :], axis=1, keepdims=True)
                scale = lax.rsqrt(square / model + epsilon)
                gate = (pre_in[at, :half] + acc[at, :half]) * scale
                up = (pre_in[at, half:] + acc[at, half:]) * scale
                out[at, :] = (jax.nn.silu(gate) * up).astype(bf16)
        else:
            piece = group // 4
            for i in range(4):
                for j in range(4):
                    there = pl.ds((i * 4 + j) * piece, piece)
                    here = pl.ds((j * 4 + i) * piece, piece)
                    out[there, :] = acc[here, :]
                    sq_out[there, :] = sq[here, :]


def pre_product(part, own, other, w_up, carried, model):
    group, depth = own[0].shape
    width = w_up.shape[-1]
    block = 512
    steps = depth // block
    low = steps // 2
    whole = pl.BlockSpec((group, block), lambda k: (0, k))
    first = pl.BlockSpec((group, block), lambda k: (0, jnp.minimum(k, low - 1)))
    second = pl.BlockSpec((group, block), lambda k: (0, jnp.maximum(k - low, 0)))
    five = [whole, whole, whole, first, second]
    last = carried is not None
    rows = 4 * group
    in_specs = five + five + [pl.BlockSpec((1, 2, block, width), lambda k: (part, 0, k, 0))]
    operands = list(own) + list(other) + [w_up]
    if last:
        in_specs += [
            pl.BlockSpec((rows, width), lambda k: (0, 0)),
            pl.BlockSpec((rows, 128), lambda k: (0, 0)),
        ]
        operands += list(carried)
        out_shape = jax.ShapeDtypeStruct((rows, width // 2), bf16)
        out_specs = pl.BlockSpec((rows, width // 2), lambda k: (0, 0))
    else:
        out_shape = (
            jax.ShapeDtypeStruct((rows, width), f32),
            jax.ShapeDtypeStruct((rows, 128), f32),
        )
        out_specs = (
            pl.BlockSpec((rows, width), lambda k: (0, 0)),
            pl.BlockSpec((rows, 128), lambda k: (0, 0)),
        )

    def kernel(*refs):
        pre_kernel(*refs, last=last, model=model)

    return pl.pallas_call(
        kernel,
        grid=(steps,),
        in_specs=in_specs,
        out_specs=out_specs,
        out_shape=out_shape,
        scratch_shapes=[
            pltpu.VMEM((rows, block), bf16),
            pltpu.VMEM((rows, block), bf16),
            pltpu.VMEM((rows, width), f32),
            pltpu.VMEM((rows, 128), f32),
        ],
        compiler_params=pltpu.CompilerParams(vmem_limit_bytes=40 * 1024 * 1024),
        cost_estimate=pl.CostEstimate(
            flops=4 * rows * depth * width,
            bytes_accessed=4 * depth * (width + rows),
            transcendentals=0,
        ),
        name="pre_last" if last else "pre_first",
    )(*operands)


def column_sums(parts):
    row = lax.broadcasted_iota(jnp.int32, parts[0].shape, 0)
    shift = 1
    while len(parts) > 1:
        keep = (row // shift) % 2 == 0
        parts = [
            jnp.where(keep, a, b) + pltpu.roll(jnp.where(keep, b, a), shift, 0)
            for a, b in zip(parts[::2], parts[1::2])
        ]
        shift *= 2
    return parts[0]


def scan_kernel(place, own, got1, got2, got3, u, zin, dt_gain, dt_weight, dt_bias, a_log, skip,
                ssm, y_out, final, step, driven, bc, b_rows, c_rows, scanned):
    seq, low_rank = u.shape[0], dt_weight.shape[0]
    states, chans = a_log.shape

    def projected(cols):
        return (
            own[:, cols]
            + got1[:, cols].astype(f32)
            + got2[:, cols].astype(f32)
            + got3[:, cols].astype(f32)
        )

    low = projected(slice(0, low_rank))
    norm = low * lax.rsqrt(jnp.mean(low * low, axis=1, keepdims=True) + epsilon)
    norm = (norm * dt_gain[...]).astype(bf16)
    bc[...] = jnp.zeros_like(bc)
    bc[:, pl.ds(0, 2 * states)] = projected(slice(low_rank, low_rank + 2 * states))
    turned = bc[...].T
    for t in range(seq):
        b_rows[pl.ds(t * states, states), :] = jnp.broadcast_to(
            turned[:states, t : t + 1], (states, 128)
        )
        c_rows[pl.ds(t * states, states), :] = jnp.broadcast_to(
            turned[states : 2 * states, t : t + 1], (states, 128)
        )
    tile = 256
    for n in range(chans // tile):
        cols = pl.ds(n * tile, tile)
        raw = jnp.dot(norm, dt_weight[:, cols], preferred_element_type=f32) + dt_bias[:, cols]
        size = jnp.maximum(raw, 0.0) + jnp.log1p(jnp.exp(-jnp.abs(raw)))
        step[:, cols] = size
        driven[:, cols] = size * u[:, cols].astype(f32)
    log2e = 1.4426950408889634
    halves = states // 8
    tiles = chans // 128
    wide = 4
    unroll = 8
    for first in range(0, tiles, wide):
        span = range(first, first + wide)
        rate = [
            [jnp.exp(a_log[pl.ds(h * 8, 8), pl.ds(j * 128, 128)]) * (-log2e) for h in range(halves)]
            for j in span
        ]
        start = tuple(
            ssm[pl.ds(h * 8, 8), pl.ds(j * 128, 128)] for j in span for h in range(halves)
        )

        def advance(block, carried, span=span, rate=rate):
            carried = list(carried)
            at_rows = pl.ds(pl.multiple_of(block * unroll, unroll), unroll)
            base = block * (unroll * states)
            parts = [[] for _ in span]
            d_rows = [step[at_rows, pl.ds(j * 128, 128)] for j in span]
            du_rows = [driven[at_rows, pl.ds(j * 128, 128)] for j in span]
            for i in range(unroll):
                at_t = [
                    pl.ds(pl.multiple_of(base + i * states + h * 8, 8), 8) for h in range(halves)
                ]
                b_t = [b_rows[at, :] for at in at_t]
                c_t = [c_rows[at, :] for at in at_t]
                for n in range(len(span)):
                    d = d_rows[n][i : i + 1]
                    du = du_rows[n][i : i + 1]
                    out = None
                    for h in range(halves):
                        at = n * halves + h
                        carried[at] = jnp.exp2(d * rate[n][h]) * carried[at] + b_t[h] * du
                        term = c_t[h] * carried[at]
                        out = term if out is None else out + term
                    parts[n].append(out)
            for n, j in enumerate(span):
                scanned[at_rows, pl.ds(j * 128, 128)] = column_sums(parts[n])
            return tuple(carried)

        end = lax.fori_loop(0, seq // unroll, advance, start)
        for n, j in enumerate(span):
            for h in range(halves):
                final[pl.ds(h * 8, 8), pl.ds(j * 128, 128)] = end[n * halves + h]
    row = lax.broadcasted_iota(jnp.int32, (seq, seq), 0)
    col = lax.broadcasted_iota(jnp.int32, (seq, seq), 1)
    tok = seq // 16
    block, inside = row // tok, row % tok
    source = ((place[0] + block // 4) % 4) * 4 + (place[1] + block % 4) % 4
    turn = jnp.where(source * tok + inside == col, 1.0, 0.0).astype(bf16)
    for n in range(chans // tile):
        cols = pl.ds(n * tile, tile)
        gate = zin[:, cols].astype(f32)
        y = (scanned[:, cols] + skip[:, cols] * u[:, cols].astype(f32)) * jax.nn.silu(gate)
        y_out[:, cols] = jnp.dot(turn, y.astype(bf16), preferred_element_type=f32).astype(bf16)


def scan_mixer(place, own, got, u, zin, dt_gain, dt_weight, dt_bias, a_log, skip, ssm):
    seq, chans = u.shape
    states = a_log.shape[0]
    vmem = pl.BlockSpec(memory_space=pltpu.VMEM)
    return pl.pallas_call(
        scan_kernel,
        in_specs=[pl.BlockSpec(memory_space=pltpu.SMEM)] + [vmem] * 12,
        out_specs=(vmem, vmem),
        out_shape=(
            jax.ShapeDtypeStruct((seq, chans), bf16),
            jax.ShapeDtypeStruct((states, chans), f32),
        ),
        scratch_shapes=[
            pltpu.VMEM((seq, chans), f32),
            pltpu.VMEM((seq, chans), f32),
            pltpu.VMEM((seq, 128), f32),
            pltpu.VMEM((seq * states, 128), f32),
            pltpu.VMEM((seq * states, 128), f32),
            pltpu.VMEM((seq, chans), f32),
        ],
        compiler_params=pltpu.CompilerParams(vmem_limit_bytes=32 * 1024 * 1024),
        cost_estimate=pl.CostEstimate(
            flops=8 * seq * states * chans,
            bytes_accessed=16 * seq * chans,
            transcendentals=seq * states * chans,
        ),
        name="scan_mixer",
    )(place, own, *got, u, zin, dt_gain, dt_weight, dt_bias, a_log, skip, ssm)


def ranks(member):
    tokens = member.shape[-1]
    before = jnp.arange(tokens)[:, None] < jnp.arange(tokens)[None, :]
    return jnp.sum(
        jnp.where(before, member[..., :, None], 0), axis=-2
    )


def conv_project(x_shard, conv_state, conv_weight, conv_bias, proj_x):
    seq_len = x_shard.shape[0]
    kernel = conv_weight.shape[0]
    extended = jnp.concatenate([conv_state[0], x_shard], axis=0).astype(f32)
    conv_pre = jnp.broadcast_to(conv_bias.astype(f32), x_shard.shape)
    for shift_pos in range(kernel):
        conv_pre = conv_pre + extended[shift_pos : shift_pos + seq_len] * conv_weight[
            shift_pos
        ].astype(f32)
    u_act = jax.nn.silu(conv_pre).astype(bf16)
    return u_act, jnp.dot(u_act, proj_x, preferred_element_type=f32)


def body(
    x_in,
    z_in,
    conv_state,
    ssm_state,
    conv_weight,
    conv_bias,
    proj_x,
    dt_gain,
    dt_weight,
    dt_bias,
    a_log,
    skip_scale,
    out_weight,
    hidden,
    moe_gain,
    router,
    routes,
    gate_codes,
    gate_zero,
    gate_scale,
    up_codes,
    up_zero,
    up_scale,
    down_codes,
    down_zero,
    down_scale,
):
    z, core = lax.axis_index("z"), lax.axis_index("core")
    gx, gy = lax.axis_index("x"), lax.axis_index("y")
    tok = x_in.shape[0]
    model = hidden.shape[1]
    experts = router.shape[1]
    cap = min(tok, (2 * tok + experts - 1) // experts + tok // 8)
    cols = model // 8
    half = cols // 2
    inner_cols = x_in.shape[1] // 16

    both = jnp.stack([x_in.reshape(tok, 16, inner_cols), z_in.reshape(tok, 16, inner_cols)])
    both = lax.all_to_all(
        both.transpose(2, 0, 1, 3), ("x", "y"), split_axis=0, concat_axis=0, tiled=True
    )
    x_shard = both[:, 0].reshape(16 * tok, inner_cols)
    z_shard = both[:, 1].reshape(16 * tok, inner_cols)

    u_act, partial = conv_project(x_shard, conv_state, conv_weight, conv_bias, proj_x)
    sent = partial.astype(bf16)
    got = [hop(sent, "y", s) for s in (1, 2, 3)]
    partial = partial + sum(g.astype(f32) for g in got)
    sent = partial.astype(bf16)
    sent, hidden, routes = lax.optimization_barrier((sent, hidden, routes))
    got = [hop(sent, "x", s) for s in (1, 2, 3)]

    hid = hidden.reshape(tok, RING, 2, cols)
    flags = jnp.pad(routes.astype(bf16), ((0, 0), (0, 126)))
    mine = jnp.concatenate([pick(hid, core, 2).reshape(tok, -1), flags], axis=1)
    theirs = jnp.concatenate([pick(hid, 1 - core, 2).reshape(tok, -1), flags], axis=1)
    pair = jnp.stack([mine, hop(theirs, "core", 1)])
    pair_cols = pair[..., : RING * cols].reshape(2, tok, RING, cols)
    pair_flags = pair[..., RING * cols :]
    pieces = [
        jnp.concatenate([pick(pair_cols, (z + d) % RING, 2), pair_flags], axis=-1)
        for d in range(RING)
    ]
    pieces = jnp.stack([pieces[0]] + [hop(pieces[d], "z", d) for d in (1, 2, 3)])
    hid_t = pieces[..., :cols].reshape(8 * tok, cols)
    route_t = pieces[..., cols : cols + 2].astype(jnp.int32)

    d_ids = jnp.arange(RING)
    k_ids = (z + d_ids) % RING
    src_z = (z - d_ids) % RING
    src_core = (core + jnp.arange(2)) % 2
    src_e = src_z[:, None] * 2 + src_core[None, :]
    member = jnp.any(
        route_t[None] == k_ids[:, None, None, None, None], axis=-1
    ).astype(jnp.int32)
    slot = src_e[None, :, :, None] * cap + ranks(member)
    slot = jnp.where(member > 0, slot, -1)
    own = jnp.where(
        src_z[None, :, None, None] == k_ids[:, None, None, None],
        8 * cap + src_core[None, None, :, None] * tok + jnp.arange(tok)[None, None, None, :],
        -1,
    )
    slot, own = slot.reshape(RING, 1, 8 * tok), own.reshape(RING, 1, 8 * tok)
    row_ids = jnp.arange(8 * cap + 2 * tok)[None, :, None]
    select = ((slot == row_ids) | (own == row_ids)).astype(bf16)

    y_rel, final_state = scan_mixer(
        jnp.stack([gx, gy]).astype(jnp.int32),
        partial,
        got,
        u_act,
        z_shard,
        dt_gain.astype(f32)[None],
        dt_weight,
        dt_bias[None],
        a_log,
        skip_scale[None],
        ssm_state[0],
    )

    y_blocks = [y_rel] + [hop(y_rel, "z", d) for d in (1, 2, 3)]
    y_all = jnp.stack([jnp.stack([b, hop(b, "core", 1)]) for b in y_blocks])
    y_all = y_all.reshape(RING, 2, RING, RING, tok, inner_cols)

    place = jnp.stack([z, core]).astype(jnp.int32)
    place, y_all = lax.optimization_barrier((place, y_all))
    gain = jnp.broadcast_to(moe_gain.astype(f32)[:, None], (model, 128))
    w_up = up_dequant(
        place,
        gate_codes[0],
        gate_zero[0],
        gate_scale[0].astype(f32),
        up_codes[0],
        up_zero[0],
        up_scale[0].astype(f32),
        gain,
    )
    w_down = down_dequant(place, down_codes[0], down_zero[0], down_scale[0].astype(f32))

    def project(rows, weight):
        rows = rows.reshape(-1, inner_cols)
        return jnp.dot(rows, weight, preferred_element_type=f32)

    def mixed(part):
        weight = out_weight[:, part * half : (part + 1) * half]
        first, second = ("y", "x") if part == 0 else ("x", "y")
        axis = 3 if part == 0 else 2
        terms = [
            project(lax.index_in_dim(y_all, s, axis, keepdims=False), weight) for s in range(RING)
        ]
        total = gather_sum(terms, first, 1).reshape(8, RING, tok, half)
        total = gather_sum([total[:, s] for s in range(RING)], second, 1)
        return total.reshape(8 * tok, half)

    def dispatched(part):
        residual = hid_t[:, part * half : (part + 1) * half].astype(f32) + mixed(part)
        rows = jnp.dot(
            select.reshape(-1, 8 * tok), residual.astype(bf16), preferred_element_type=f32
        ).astype(bf16).reshape(RING, -1, half)
        arrived = [rows[0]] + [hop(rows[d], "z", d) for d in (1, 2, 3)]
        routed = jnp.concatenate([a[: 8 * cap] for a in arrived], axis=1)
        kept = jnp.stack([a[8 * cap :] for a in arrived])
        return routed, kept

    def gathered(part, routed):
        first, second = ("x", "y") if part == 0 else ("y", "x")
        near = jnp.concatenate(spread(routed, first), axis=0)
        behind, ahead = hop(near, second, 1), hop(near, second, -1)
        split = near.shape[-1] // 2
        groups = [
            near,
            behind,
            ahead,
            hop(behind[:, :split], second, 1),
            hop(ahead[:, split:], second, -1),
        ]
        return groups, [hop(g, "core", 1) for g in groups]

    routed_0, kept_0 = dispatched(0)
    routed_1, kept_1 = dispatched(1)
    own_0, other_0 = gathered(0, routed_0)
    own_1, other_1 = gathered(1, routed_1)
    carried = pre_product(0, own_0, other_0, w_up, None, model)
    inner_act = pre_product(1, own_1, other_1, w_up, carried, model)
    units = inner_act.shape[-1]
    inner_act = inner_act.reshape(RING, RING, 8 * cap, units)

    def expert_sum(part):
        first, second = ("y", "x") if part == 0 else ("x", "y")
        axis = 1 if part == 0 else 0
        terms = []
        for s in range(RING):
            rows = lax.index_in_dim(inner_act, s, axis, keepdims=False).reshape(-1, units)
            away = jnp.dot(rows, w_down[1, part], preferred_element_type=f32).astype(bf16)
            here = jnp.dot(rows, w_down[0, part], preferred_element_type=f32)
            terms.append(here + hop(away, "core", 1).astype(f32))
        total = gather_sum(terms, first, -1).reshape(RING, 8 * cap, -1)
        return gather_sum([total[s] for s in range(RING)], second, -1).astype(bf16)

    sums = jnp.concatenate([expert_sum(0), expert_sum(1)], axis=1).reshape(RING, 2 * cap, -1)
    back = [pick(sums, (z + d) % RING, 0) for d in range(RING)]
    back = jnp.stack([back[0]] + [hop(back[d], "z", d) for d in (1, 2, 3)])
    back = back.reshape(RING, 2, cap, -1)
    back_own = pick(back, core, 1).reshape(RING * cap, -1)
    back_other = hop(pick(back, 1 - core, 1), "core", 1).reshape(RING * cap, -1)

    kept = jnp.concatenate([kept_0, kept_1], axis=-1).reshape(RING, 2, tok, cols)
    res_own = pick(kept, core, 1)
    res_other = hop(pick(kept, 1 - core, 1), "core", 1)

    def ordered(own_part, other_part):
        low = jnp.where(core == 0, own_part, other_part)
        high = jnp.where(core == 0, other_part, own_part)
        return jnp.stack([low, high], axis=1).transpose(2, 0, 1, 3).reshape(tok, model)

    def absolute(value):
        return jnp.stack([pick(value, (z - i) % RING, 0) for i in range(RING)])

    residual = ordered(absolute(res_own), absolute(res_other)).astype(f32)
    normed = (
        residual
        * lax.rsqrt(jnp.mean(residual * residual, axis=1, keepdims=True) + epsilon)
        * moe_gain.astype(f32)
    ).astype(bf16)
    logits = jnp.dot(normed, router, preferred_element_type=f32)
    weights = jnp.exp(logits)
    probs = weights / jnp.sum(weights, axis=1, keepdims=True)
    named = jnp.any(routes[None] == jnp.arange(experts)[:, None, None], axis=-1)
    rank = ranks(named.astype(jnp.int32))
    gates = jnp.where(
        named[:, :, None] & (rank[:, :, None] == jnp.arange(cap)), probs.T[:, :, None], 0.0
    )
    gates = jnp.stack([pick(gates, (z - d) % RING, 0) for d in range(RING)])
    gates = gates.transpose(1, 0, 2).reshape(tok, RING * cap)

    def combined(rows):
        out = jnp.dot(gates, rows.astype(f32), precision=lax.Precision.HIGHEST)
        return out.reshape(tok, 2, RING, half).transpose(2, 0, 1, 3).reshape(RING, tok, cols)

    layer_out = (residual + ordered(combined(back_own), combined(back_other))).astype(bf16)
    return (layer_out, final_state[None])


def solution(mesh):
    fine = Mesh(mesh.devices.reshape(RING, 2, RING, RING), ("z", "core", "x", "y"))
    e, c = ("z", "core"), ("x", "y")
    every = e + c
    return jax.shard_map(
        body,
        mesh=fine,
        in_specs=(
            P(every, None),
            P(every, None),
            P(e, None, c),
            P(e, None, c),
            P(None, c),
            P(c),
            P(c, None),
            P(),
            P(None, c),
            P(c),
            P(None, c),
            P(c),
            P(c, e),
            P(every, None),
            P(),
            P(),
            P(every, None),
            P(e, None, c),
            P(e, None, c),
            P(e, None, c),
            P(e, None, c),
            P(e, None, c),
            P(e, None, c),
            P(e, c, None),
            P(e, c, None),
            P(e, c, None),
        ),
        out_specs=(P(every, None), P(e, None, c)),
        check_vma=False,
    )
```

```python
import jax
import jax.numpy as jnp
from jax import lax
from jax.experimental import pallas as pl
from jax.experimental.pallas import tpu as pltpu
from jax.sharding import Mesh, PartitionSpec as P

epsilon = 1e-05
f32 = jnp.float32
bf16 = jnp.bfloat16
RING = 4


def hop(value, axis, step):
    size = lax.axis_size(axis)
    return lax.ppermute(value, axis, [(i, (i + step) % size) for i in range(size)])


def pick(value, index, axis):
    return lax.dynamic_index_in_dim(value, index, axis, keepdims=False)


def pinned(value):
    return pltpu.with_memory_space_constraint(value, pltpu.HBM)


def together(*values):
    return lax.optimization_barrier(values)


def gather_sum(terms, axis, sign):
    total = terms[0].astype(f32)
    arrived = [hop(terms[s].astype(bf16), axis, sign * s) for s in (1, 2, 3)]
    for term in arrived:
        total = total + term.astype(f32)
    return total


def ring_sums(across, others, axes, sign):
    half = across[0].shape[0] // 2
    sent = together(*[side for a in across for side in (a[:half], a[half:])])
    low = [hop(sent[2 * p], axes[p], sign) for p in range(2)]
    high = [hop(sent[2 * p + 1], axes[p], -sign) for p in range(2)]
    others = others()
    passed = []
    for p in range(2):
        ahead, behind = others[p][1].astype(f32), others[p][2].astype(f32)
        ahead = jnp.concatenate([ahead[:half] + low[p].astype(f32), ahead[half:]], axis=0)
        behind = jnp.concatenate([behind[:half], behind[half:] + high[p].astype(f32)], axis=0)
        passed += [ahead.astype(bf16), behind.astype(bf16)]
    *passed, first_0, first_1 = together(*passed, *[o[0].astype(f32) for o in others])
    got = [
        (hop(passed[2 * p], axes[p], sign), hop(passed[2 * p + 1], axes[p], -sign))
        for p in range(2)
    ]
    return [
        first + got[p][0].astype(f32) + got[p][1].astype(f32)
        for p, first in enumerate((first_0, first_1))
    ]


def up_dequant_kernel(place, gc, gz, gs, uc, uz, us, gain, out):
    rows = gc.shape[0]
    groups = gz.shape[0]
    size = rows // groups
    width = gc.shape[1]
    half = groups // 2
    for codes, zero, scale, at in ((gc, gz, gs, 0), (uc, uz, us, width)):
        for g in range(groups):
            values = codes[pl.ds(g * size, size), :].astype(f32) - zero[pl.ds(g, 1), :].astype(f32)
            values = values * scale[pl.ds(g, 1), :]
            weight = gain[pl.ds(g * size, size), :]
            for lane in range(width // 128):
                out[g // half, 0, pl.ds((g % half) * size, size), pl.ds(at + lane * 128, 128)] = (
                    values[:, lane * 128 : (lane + 1) * 128] * weight
                ).astype(bf16)


def up_dequant(place, codes_a, zero_a, scale_a, codes_b, zero_b, scale_b, gain):
    model, width = codes_a.shape
    block = model // 8
    groups = zero_a.shape[0] // 8

    def source(dc, d, place):
        return (lax.rem(place[0] - d + RING, RING) * 2 + lax.rem(place[1] + dc, 2), 0)

    code_spec = pl.BlockSpec((block, width), source)
    group_spec = pl.BlockSpec((groups, width), source)
    return pl.pallas_call(
        up_dequant_kernel,
        grid_spec=pltpu.PrefetchScalarGridSpec(
            num_scalar_prefetch=1,
            grid=(2, RING),
            in_specs=[
                code_spec,
                group_spec,
                group_spec,
                code_spec,
                group_spec,
                group_spec,
                pl.BlockSpec((block, 128), source),
            ],
            out_specs=pl.BlockSpec(
                (2, 1, block // 2, 2 * width), lambda dc, d, place: (0, dc, d, 0)
            ),
        ),
        out_shape=pltpu.HBM((2, 2, model // 4, 2 * width), bf16),
        compiler_params=pltpu.CompilerParams(vmem_limit_bytes=20 * 1024 * 1024),
        cost_estimate=pl.CostEstimate(
            flops=8 * model * width, bytes_accessed=10 * model * width, transcendentals=0
        ),
        name="up_dequant",
    )(place, pinned(codes_a), zero_a, scale_a, pinned(codes_b), zero_b, scale_b, gain)


def down_dequant_kernel(place, codes, zero, scale, out):
    groups = zero.shape[0]
    size = codes.shape[0] // groups
    half = codes.shape[1] // 2
    for g in range(groups):
        rows = pl.ds(g * size, size)
        for part in range(2):
            cols = pl.ds(part * half, half)
            values = codes[rows, cols].astype(f32) - zero[pl.ds(g, 1), cols].astype(f32)
            out[0, part, rows, :] = (values * scale[pl.ds(g, 1), cols]).astype(bf16)


def down_dequant(place, codes, zero, scale):
    rows, model = codes.shape
    block = model // 8
    groups = zero.shape[0]

    def source(dc, d, place):
        return (0, d * 2 + lax.rem(place[1] + dc, 2))

    return pl.pallas_call(
        down_dequant_kernel,
        grid_spec=pltpu.PrefetchScalarGridSpec(
            num_scalar_prefetch=1,
            grid=(2, RING),
            in_specs=[
                pl.BlockSpec((rows, block), source),
                pl.BlockSpec((groups, block), source),
                pl.BlockSpec((groups, block), source),
            ],
            out_specs=pl.BlockSpec(
                (1, 2, rows, block // 2), lambda dc, d, place: (dc, 0, 0, d)
            ),
        ),
        out_shape=jax.ShapeDtypeStruct((2, 2, rows, model // 4), bf16),
        compiler_params=pltpu.CompilerParams(vmem_limit_bytes=20 * 1024 * 1024),
        cost_estimate=pl.CostEstimate(
            flops=3 * model * rows, bytes_accessed=4 * model * rows, transcendentals=0
        ),
        name="down_dequant",
    )(place, pinned(codes), zero, scale)


def pre_kernel(*refs, counts, last, model):
    sources, rest = refs[: sum(counts)], refs[sum(counts) :]
    w = rest[0]
    if last:
        pre_in, sq_in, out, rows, acc, sq, full, full_sq = rest[1:]
    else:
        out, sq_out, rows, acc, sq = rest[1:]
    part, k = pl.program_id(0), pl.program_id(1)
    steps = pl.num_programs(1)
    block = w.shape[2]
    width = w.shape[3]
    group = (pre_in if last else out).shape[0] // RING
    groups = rows.shape[0] // group
    per_side = counts[0] // 2

    for p in range(2):
        for side in range(2):
            first = p * counts[0] + side * per_side
            mine = sources[first : first + per_side]
            cols = pl.ds(side * block, block)
            @pl.when(part == p)
            def _(mine=mine, cols=cols):
                size = mine[0].shape[0]
                for g, source in enumerate(mine):
                    rows[pl.ds(g * size, size), cols] = source[...]

    product = jnp.dot(
        rows[...], w[0].reshape(2 * block, width), preferred_element_type=f32
    )

    def squares(at):
        total = None
        for j in range(2 * block // 128):
            v = rows[at, pl.ds(j * 128, 128)].astype(f32)
            total = v * v if total is None else total + v * v
        return total

    @pl.when(k == 0)
    def _():
        acc[part] = product
        for g in range(groups):
            at = pl.ds(g * group, group)
            sq[part, at, :] = squares(at)

    @pl.when(k > 0)
    def _():
        acc[part] += product
        for g in range(groups):
            at = pl.ds(g * group, group)
            sq[part, at, :] += squares(at)

    piece = group // RING

    @pl.when((part == 1) & (k == steps - 1))
    def _():
        if last:
            full[...] = pre_in[...]
            full_sq[...] = sq_in[...]
            for i in range(RING):
                down = pl.ds((i * RING + 2) * piece, piece)
                along = pl.ds((2 * RING + i) * piece, piece)
                here = pl.ds(i * piece, piece)
                full[down, :] += acc[0, here, :]
                full_sq[down, :] += sq[0, here, :]
                full[along, :] += acc[1, here, :]
                full_sq[along, :] += sq[1, here, :]
            half = width // 2
            for r in range(RING):
                at = pl.ds(r * group, group)
                square = jnp.sum(full_sq[at, :], axis=1, keepdims=True)
                scale = lax.rsqrt(square / model + epsilon)
                gate = full[at, :half] * scale
                up = full[at, half:] * scale
                out[at, :] = (jax.nn.silu(gate) * up).astype(bf16)
        else:
            place = {0: 0, 1: 1, 3: 2}
            for i in range(RING):
                for j in range(RING):
                    there = pl.ds((i * RING + j) * piece, piece)
                    total, total_sq = None, None
                    for p, major, minor in ((0, j, i), (1, i, j)):
                        if major == 2:
                            continue
                        here = pl.ds(place[major] * group + minor * piece, piece)
                        term, term_sq = acc[p, here, :], sq[p, here, :]
                        total = term if total is None else total + term
                        total_sq = term_sq if total_sq is None else total_sq + term_sq
                    if total is None:
                        total = jnp.zeros((piece, width), f32)
                        total_sq = jnp.zeros((piece, 128), f32)
                    out[there, :] = total
                    sq_out[there, :] = total_sq


def pre_product(parts, w_up, carried, model):
    last = carried is not None
    block_rows = parts[0][0][0].shape[0]
    group = block_rows * 2 if last else block_rows
    width = w_up.shape[-1]
    depth = w_up.shape[2]
    block = 1024
    steps = depth // block
    counts = tuple(len(own) + len(other) for own, other in parts)
    in_specs, operands = [], []
    for p, sides in enumerate(parts):
        for side in sides:
            for array in side:

                def index(part, k, p=p):
                    return (0, jnp.where(part == p, k, 0 if p else steps - 1))

                in_specs.append(pl.BlockSpec((block_rows, block), index))
                operands.append(array)
    in_specs.append(pl.BlockSpec((1, 2, block, width), lambda part, k: (part, 0, k, 0)))
    operands.append(w_up)
    total = RING * group
    rows = group if last else 3 * group

    def whole(*shape):
        return pl.BlockSpec(shape, lambda part, k: (0, 0))

    scratch = [
        pltpu.VMEM((rows, 2 * block), bf16),
        pltpu.VMEM((2, rows, width), f32),
        pltpu.VMEM((2, rows, 128), f32),
    ]
    if last:
        in_specs += [whole(total, width), whole(total, 128)]
        operands += list(carried)
        out_shape = jax.ShapeDtypeStruct((total, width // 2), bf16)
        out_specs = whole(total, width // 2)
        scratch += [pltpu.VMEM((total, width), f32), pltpu.VMEM((total, 128), f32)]
    else:
        out_shape = (
            jax.ShapeDtypeStruct((total, width), f32),
            jax.ShapeDtypeStruct((total, 128), f32),
        )
        out_specs = (whole(total, width), whole(total, 128))

    def kernel(*refs):
        pre_kernel(*refs, counts=counts, last=last, model=model)

    return pl.pallas_call(
        kernel,
        grid=(2, steps),
        in_specs=in_specs,
        out_specs=out_specs,
        out_shape=out_shape,
        scratch_shapes=scratch,
        compiler_params=pltpu.CompilerParams(vmem_limit_bytes=30 * 1024 * 1024),
        cost_estimate=pl.CostEstimate(
            flops=8 * rows * depth * width,
            bytes_accessed=8 * depth * (width + rows),
            transcendentals=0,
        ),
        name="pre_last" if last else "pre_first",
    )(*operands)


def column_sums(parts):
    row = lax.broadcasted_iota(jnp.int32, parts[0].shape, 0)
    shift = 1
    while len(parts) > 1:
        keep = (row // shift) % 2 == 0
        parts = [
            jnp.where(keep, a, b) + pltpu.roll(jnp.where(keep, b, a), shift, 0)
            for a, b in zip(parts[::2], parts[1::2])
        ]
        shift *= 2
    return parts[0]


def scan_kernel(own, got1, got2, got3, u, zin, dt_gain, dt_weight, dt_bias, a_log, skip,
                ssm, y_out, final, step, driven, bc, b_rows, c_rows, scanned):
    seq, low_rank = u.shape[0], dt_weight.shape[0]
    states, chans = a_log.shape

    def projected(cols):
        return (
            own[:, cols]
            + got1[:, cols].astype(f32)
            + got2[:, cols].astype(f32)
            + got3[:, cols].astype(f32)
        )

    low = projected(slice(0, low_rank))
    norm = low * lax.rsqrt(jnp.mean(low * low, axis=1, keepdims=True) + epsilon)
    norm = (norm * dt_gain[...]).astype(bf16)
    bc[...] = jnp.zeros_like(bc)
    bc[:, pl.ds(0, 2 * states)] = projected(slice(low_rank, low_rank + 2 * states))
    turned = bc[...].T
    for t in range(seq):
        b_rows[pl.ds(t * states, states), :] = jnp.broadcast_to(
            turned[:states, t : t + 1], (states, 128)
        )
        c_rows[pl.ds(t * states, states), :] = jnp.broadcast_to(
            turned[states : 2 * states, t : t + 1], (states, 128)
        )
    tile = 256
    for n in range(chans // tile):
        cols = pl.ds(n * tile, tile)
        raw = jnp.dot(norm, dt_weight[:, cols], preferred_element_type=f32) + dt_bias[:, cols]
        size = jnp.maximum(raw, 0.0) + jnp.log1p(jnp.exp(-jnp.abs(raw)))
        step[:, cols] = size
        driven[:, cols] = size * u[:, cols].astype(f32)
    log2e = 1.4426950408889634
    halves = states // 8
    tiles = chans // 128
    wide = 4
    unroll = 8
    for first in range(0, tiles, wide):
        span = range(first, first + wide)
        rate = [
            [jnp.exp(a_log[pl.ds(h * 8, 8), pl.ds(j * 128, 128)]) * (-log2e) for h in range(halves)]
            for j in span
        ]
        start = tuple(
            ssm[pl.ds(h * 8, 8), pl.ds(j * 128, 128)] for j in span for h in range(halves)
        )

        def advance(block, carried, span=span, rate=rate):
            carried = list(carried)
            at_rows = pl.ds(pl.multiple_of(block * unroll, unroll), unroll)
            base = block * (unroll * states)
            parts = [[] for _ in span]
            d_rows = [step[at_rows, pl.ds(j * 128, 128)] for j in span]
            du_rows = [driven[at_rows, pl.ds(j * 128, 128)] for j in span]
            for i in range(unroll):
                at_t = [
                    pl.ds(pl.multiple_of(base + i * states + h * 8, 8), 8) for h in range(halves)
                ]
                b_t = [b_rows[at, :] for at in at_t]
                c_t = [c_rows[at, :] for at in at_t]
                for n in range(len(span)):
                    d = d_rows[n][i : i + 1]
                    du = du_rows[n][i : i + 1]
                    out = None
                    for h in range(halves):
                        at = n * halves + h
                        carried[at] = jnp.exp2(d * rate[n][h]) * carried[at] + b_t[h] * du
                        term = c_t[h] * carried[at]
                        out = term if out is None else out + term
                    parts[n].append(out)
            for n, j in enumerate(span):
                scanned[at_rows, pl.ds(j * 128, 128)] = column_sums(parts[n])
            return tuple(carried)

        end = lax.fori_loop(0, seq // unroll, advance, start)
        for n, j in enumerate(span):
            for h in range(halves):
                final[pl.ds(h * 8, 8), pl.ds(j * 128, 128)] = end[n * halves + h]
    for n in range(chans // tile):
        cols = pl.ds(n * tile, tile)
        gate = zin[:, 1, :, cols].astype(f32).reshape(seq, tile)
        y = (scanned[:, cols] + skip[:, cols] * u[:, cols].astype(f32)) * jax.nn.silu(gate)
        y_out[:, cols] = y.astype(bf16)


def scan_mixer(own, got, u, zin, dt_gain, dt_weight, dt_bias, a_log, skip, ssm):
    seq, chans = u.shape
    states = a_log.shape[0]
    vmem = pl.BlockSpec(memory_space=pltpu.VMEM)
    return pl.pallas_call(
        scan_kernel,
        in_specs=[vmem] * 12,
        out_specs=(vmem, vmem),
        out_shape=(
            jax.ShapeDtypeStruct((seq, chans), bf16),
            jax.ShapeDtypeStruct((states, chans), f32),
        ),
        scratch_shapes=[
            pltpu.VMEM((seq, chans), f32),
            pltpu.VMEM((seq, chans), f32),
            pltpu.VMEM((seq, 128), f32),
            pltpu.VMEM((seq * states, 128), f32),
            pltpu.VMEM((seq * states, 128), f32),
            pltpu.VMEM((seq, chans), f32),
        ],
        compiler_params=pltpu.CompilerParams(vmem_limit_bytes=20 * 1024 * 1024),
        cost_estimate=pl.CostEstimate(
            flops=8 * seq * states * chans,
            bytes_accessed=16 * seq * chans,
            transcendentals=seq * states * chans,
        ),
        name="scan_mixer",
    )(own, *got, u, zin, dt_gain, dt_weight, dt_bias, a_log, skip, ssm)


def ranks(member):
    tokens = member.shape[-1]
    before = jnp.arange(tokens)[:, None] < jnp.arange(tokens)[None, :]
    return jnp.sum(
        jnp.where(before, member[..., :, None], 0), axis=-2
    )


def conv_project(x_shard, conv_state, conv_weight, conv_bias, proj_x):
    seq_len = x_shard.shape[0]
    kernel = conv_weight.shape[0]
    extended = jnp.concatenate([conv_state[0], x_shard], axis=0).astype(f32)
    conv_pre = jnp.broadcast_to(conv_bias.astype(f32), x_shard.shape)
    for shift_pos in range(kernel):
        conv_pre = conv_pre + extended[shift_pos : shift_pos + seq_len] * conv_weight[
            shift_pos
        ].astype(f32)
    u_act = jax.nn.silu(conv_pre).astype(bf16)
    return u_act, jnp.dot(u_act, proj_x, preferred_element_type=f32)


def body(
    x_in,
    z_in,
    conv_state,
    ssm_state,
    conv_weight,
    conv_bias,
    proj_x,
    dt_gain,
    dt_weight,
    dt_bias,
    a_log,
    skip_scale,
    out_weight,
    hidden,
    moe_gain,
    router,
    routes,
    gate_codes,
    gate_zero,
    gate_scale,
    up_codes,
    up_zero,
    up_scale,
    down_codes,
    down_zero,
    down_scale,
):
    z, core = lax.axis_index("z"), lax.axis_index("core")
    tok = x_in.shape[0]
    model = hidden.shape[1]
    experts = router.shape[1]
    cap = min(tok, (2 * tok + experts - 1) // experts + tok // 8)
    cols = model // 8
    half = cols // 2
    inner_cols = x_in.shape[1] // 16

    both = jnp.stack([x_in.reshape(tok, 16, inner_cols), z_in.reshape(tok, 16, inner_cols)])
    both, hidden = together(both.transpose(2, 0, 1, 3), hidden)
    both = lax.all_to_all(both, ("x", "y"), split_axis=0, concat_axis=0, tiled=True)
    hid = hidden.reshape(tok, RING, 2, cols)
    flags = jnp.pad(routes.astype(bf16), ((0, 0), (0, 126)))
    mine = jnp.concatenate([pick(hid, core, 2).reshape(tok, -1), flags], axis=1)
    theirs = jnp.concatenate([pick(hid, 1 - core, 2).reshape(tok, -1), flags], axis=1)
    pair = jnp.stack([mine, hop(theirs, "core", 1)])
    pair_cols = pair[..., : RING * cols].reshape(2, tok, RING, cols)
    pair_flags = pair[..., RING * cols :]
    pieces = [
        jnp.concatenate([pick(pair_cols, (z + d) % RING, 2), pair_flags], axis=-1)
        for d in range(RING)
    ]
    pieces = jnp.stack([pieces[0]] + [hop(pieces[d], "z", d) for d in (1, 2, 3)])
    conv_state, pieces = together(conv_state, pieces)
    hid_t = pieces[..., :cols].reshape(8 * tok, cols)
    route_t = pieces[..., cols : cols + 2].astype(jnp.int32)

    x_shard = both[:, 0].reshape(16 * tok, inner_cols)

    u_act, partial = conv_project(x_shard, conv_state, conv_weight, conv_bias, proj_x)
    sent = partial.astype(bf16)
    got = [hop(sent, "y", s) for s in (1, 2, 3)]
    partial = partial + sum(g.astype(f32) for g in got)
    sent = partial.astype(bf16)
    got = [hop(sent, "x", s) for s in (1, 2, 3)]

    d_ids = jnp.arange(RING)
    k_ids = (z + d_ids) % RING
    src_z = (z - d_ids) % RING
    src_core = (core + jnp.arange(2)) % 2
    src_e = src_z[:, None] * 2 + src_core[None, :]
    member = jnp.any(
        route_t[None] == k_ids[:, None, None, None, None], axis=-1
    ).astype(jnp.int32)
    slot = src_e[None, :, :, None] * cap + ranks(member)
    slot = jnp.where(member > 0, slot, -1)
    own = jnp.where(
        src_z[None, :, None, None] == k_ids[:, None, None, None],
        8 * cap + src_core[None, None, :, None] * tok + jnp.arange(tok)[None, None, None, :],
        -1,
    )
    slot, own = slot.reshape(RING, 1, 8 * tok), own.reshape(RING, 1, 8 * tok)
    row_ids = jnp.arange(8 * cap + 2 * tok)[None, :, None]
    select = ((slot == row_ids) | (own == row_ids)).astype(bf16)

    y_out, final_state = scan_mixer(
        partial,
        got,
        u_act,
        both,
        dt_gain.astype(f32)[None],
        dt_weight,
        dt_bias[None],
        a_log,
        skip_scale[None],
        ssm_state[0],
    )

    blocks = [y_out] + [hop(y_out, "z", d) for d in (1, 2, 3)]
    blocks = [side for b in blocks for side in (b, hop(b, "core", 1))]
    y_all = jnp.concatenate([b.reshape(16, 1, tok, inner_cols) for b in blocks], axis=1)
    mixed = jnp.dot(
        y_all.reshape(-1, inner_cols), out_weight, preferred_element_type=f32
    ).astype(bf16)

    place = jnp.stack([z, core]).astype(jnp.int32)
    place, mixed = together(place, mixed)
    gain = jnp.broadcast_to(moe_gain.astype(f32)[:, None], (model, 128))
    w_up = up_dequant(
        place,
        gate_codes[0],
        gate_zero[0],
        gate_scale[0].astype(f32),
        up_codes[0],
        up_zero[0],
        up_scale[0].astype(f32),
        gain,
    )
    w_down = down_dequant(place, down_codes[0], down_zero[0], down_scale[0].astype(f32))

    mixed = lax.all_to_all(
        mixed.reshape(16, 8 * tok, cols), ("x", "y"), split_axis=0, concat_axis=0, tiled=True
    )
    mixed, w_up, w_down = together(mixed, w_up, w_down)

    rows = (hid_t.astype(f32) + jnp.sum(mixed.astype(f32), axis=0)).astype(bf16)
    rows = jnp.dot(select.reshape(-1, 8 * tok), rows, preferred_element_type=f32)
    rows = rows.astype(bf16).reshape(RING, -1, cols)
    arrived = [rows[0]] + [hop(rows[d], "z", d) for d in (1, 2, 3)]
    kept = jnp.stack([a[8 * cap :] for a in arrived]).reshape(RING, 2, tok, cols)

    def routed(part):
        return jnp.concatenate(
            [a[: 8 * cap, part * half : (part + 1) * half] for a in arrived], axis=1
        )

    def near(block, axis):
        return jnp.concatenate([block] + [hop(block, axis, d) for d in (1, 2, 3)], axis=0)

    routed_0, routed_1 = together(routed(0), routed(1))
    nears = together(near(routed_0, "x"), near(routed_1, "y"))
    axes = ("y", "x")
    behind = [hop(n, axis, 1) for n, axis in zip(nears, axes)]
    ahead = [hop(n, axis, -1) for n, axis in zip(nears, axes)]
    split = nears[0].shape[0] // 2
    passed = together(*[b[:split] for b in behind], *[a[split:] for a in ahead])
    across = [hop(passed[p], axes[p], 1) for p in range(2)]
    across += [hop(passed[2 + p], axes[p], -1) for p in range(2)]
    close = [[nears[p], behind[p], ahead[p]] for p in range(2)]
    carried = pre_product(
        [(own, [hop(c, "core", 1) for c in own]) for own in close], pinned(w_up), None, model
    )
    *across, pre_part, square_part = together(*across, *carried)
    last = [[across[p], across[2 + p]] for p in range(2)]
    inner_act = pre_product(
        [(own, [hop(c, "core", 1) for c in own]) for own in last],
        w_up,
        (pre_part, square_part),
        model,
    )
    units = inner_act.shape[-1]
    inner_act = inner_act.reshape(RING, RING, 8 * cap, units)

    def output(part, s):
        rows = lax.index_in_dim(inner_act, s, 1 if part == 0 else 0, keepdims=False)
        rows = rows.reshape(-1, units)
        away = jnp.dot(rows, w_down[1, part], preferred_element_type=f32).astype(bf16)
        here = jnp.dot(rows, w_down[0, part], preferred_element_type=f32)
        return here + hop(away, "core", 1).astype(f32)

    total_0, total_1 = ring_sums(
        [output(part, 2).astype(bf16) for part in range(2)],
        lambda: [[output(part, s) for s in (0, 1, 3)] for part in range(2)],
        ("y", "x"),
        -1,
    )
    total_0 = total_0.reshape(RING, 8 * cap, -1)
    total_1 = total_1.reshape(RING, 8 * cap, -1)
    terms = together(
        *[total[s].astype(bf16 if s else f32) for total in (total_0, total_1) for s in range(RING)]
    )
    total_0 = gather_sum(terms[:RING], "x", -1).astype(bf16)
    total_1 = gather_sum(terms[RING:], "y", -1).astype(bf16)
    sums = jnp.concatenate([total_0, total_1], axis=1).reshape(RING, 2 * cap, -1)
    back = [pick(sums, (z + d) % RING, 0) for d in range(RING)]
    back = jnp.stack([back[0]] + [hop(back[d], "z", d) for d in (1, 2, 3)])
    back = back.reshape(RING, 2, cap, -1)
    back_own = pick(back, core, 1).reshape(RING * cap, -1)
    back_other = hop(pick(back, 1 - core, 1), "core", 1).reshape(RING * cap, -1)

    res_own = pick(kept, core, 1)
    res_other = hop(pick(kept, 1 - core, 1), "core", 1)

    def ordered(own_part, other_part):
        low = jnp.where(core == 0, own_part, other_part)
        high = jnp.where(core == 0, other_part, own_part)
        return jnp.stack([low, high], axis=1).transpose(2, 0, 1, 3).reshape(tok, model)

    def absolute(value):
        return jnp.stack([pick(value, (z - i) % RING, 0) for i in range(RING)])

    residual = ordered(absolute(res_own), absolute(res_other)).astype(f32)
    normed = (
        residual
        * lax.rsqrt(jnp.mean(residual * residual, axis=1, keepdims=True) + epsilon)
        * moe_gain.astype(f32)
    ).astype(bf16)
    logits = jnp.dot(normed, router, preferred_element_type=f32)
    weights = jnp.exp(logits)
    probs = weights / jnp.sum(weights, axis=1, keepdims=True)
    named = jnp.any(routes[None] == jnp.arange(experts)[:, None, None], axis=-1)
    rank = ranks(named.astype(jnp.int32))
    gates = jnp.where(
        named[:, :, None] & (rank[:, :, None] == jnp.arange(cap)), probs.T[:, :, None], 0.0
    )
    gates = jnp.stack([pick(gates, (z - d) % RING, 0) for d in range(RING)])
    gates = gates.transpose(1, 0, 2).reshape(tok, RING * cap)

    def combined(rows):
        out = jnp.dot(gates, rows.astype(f32), precision=lax.Precision.HIGHEST)
        return out.reshape(tok, 2, RING, half).transpose(2, 0, 1, 3).reshape(RING, tok, cols)

    layer_out = (residual + ordered(combined(back_own), combined(back_other))).astype(bf16)
    return (layer_out, final_state[None])


def solution(mesh):
    fine = Mesh(mesh.devices.reshape(RING, 2, RING, RING), ("z", "core", "x", "y"))
    e, c = ("z", "core"), ("x", "y")
    every = e + c
    return jax.shard_map(
        body,
        mesh=fine,
        in_specs=(
            P(every, None),
            P(every, None),
            P(e, None, c),
            P(e, None, c),
            P(None, c),
            P(c),
            P(c, None),
            P(),
            P(None, c),
            P(c),
            P(None, c),
            P(c),
            P(c, e),
            P(every, None),
            P(),
            P(),
            P(every, None),
            P(e, None, c),
            P(e, None, c),
            P(e, None, c),
            P(e, None, c),
            P(e, None, c),
            P(e, None, c),
            P(e, c, None),
            P(e, c, None),
            P(e, c, None),
        ),
        out_specs=(P(every, None), P(e, None, c)),
        check_vma=False,
    )
```

```python
import jax
import jax.numpy as jnp
from jax import lax
from jax.experimental import pallas as pl
from jax.experimental.pallas import tpu as pltpu
from jax.sharding import Mesh, PartitionSpec as P

epsilon = 1e-05
f32 = jnp.float32
bf16 = jnp.bfloat16
RING = 4


def hop(value, axis, step):
    size = lax.axis_size(axis)
    return lax.ppermute(value, axis, [(i, (i + step) % size) for i in range(size)])


def pick(value, index, axis):
    return lax.dynamic_index_in_dim(value, index, axis, keepdims=False)


def pinned(value):
    return pltpu.with_memory_space_constraint(value, pltpu.HBM)


def together(*values):
    return lax.optimization_barrier(values)


def gather_sum(terms, axis, sign):
    total = terms[0].astype(f32)
    arrived = [hop(terms[s].astype(bf16), axis, sign * s) for s in (1, 2, 3)]
    for term in arrived:
        total = total + term.astype(f32)
    return total


def ring_sums(across, others, axes, sign):
    half = across[0].shape[0] // 2
    sent = together(*[side for a in across for side in (a[:half], a[half:])])
    low = [hop(sent[2 * p], axes[p], sign) for p in range(2)]
    high = [hop(sent[2 * p + 1], axes[p], -sign) for p in range(2)]
    others = others()
    passed = []
    for p in range(2):
        ahead, behind = others[p][1].astype(f32), others[p][2].astype(f32)
        ahead = jnp.concatenate([ahead[:half] + low[p].astype(f32), ahead[half:]], axis=0)
        behind = jnp.concatenate([behind[:half], behind[half:] + high[p].astype(f32)], axis=0)
        passed += [ahead.astype(bf16), behind.astype(bf16)]
    *passed, first_0, first_1 = together(*passed, *[o[0].astype(f32) for o in others])
    got = [
        (hop(passed[2 * p], axes[p], sign), hop(passed[2 * p + 1], axes[p], -sign))
        for p in range(2)
    ]
    return [
        first + got[p][0].astype(f32) + got[p][1].astype(f32)
        for p, first in enumerate((first_0, first_1))
    ]


def up_dequant_kernel(place, gc, gz, gs, uc, uz, us, gain, out):
    rows = gc.shape[0]
    groups = gz.shape[0]
    size = rows // groups
    width = gc.shape[1]
    half = groups // 2
    for codes, zero, scale, at in ((gc, gz, gs, 0), (uc, uz, us, width)):
        for g in range(groups):
            values = codes[pl.ds(g * size, size), :].astype(f32) - zero[pl.ds(g, 1), :].astype(f32)
            values = values * scale[pl.ds(g, 1), :]
            weight = gain[pl.ds(g * size, size), :]
            for lane in range(width // 128):
                out[g // half, 0, pl.ds((g % half) * size, size), pl.ds(at + lane * 128, 128)] = (
                    values[:, lane * 128 : (lane + 1) * 128] * weight
                ).astype(bf16)


def up_dequant(place, codes_a, zero_a, scale_a, codes_b, zero_b, scale_b, gain):
    model, width = codes_a.shape
    block = model // 8
    groups = zero_a.shape[0] // 8

    def source(dc, d, place):
        return (lax.rem(place[0] - d + RING, RING) * 2 + lax.rem(place[1] + dc, 2), 0)

    code_spec = pl.BlockSpec((block, width), source)
    group_spec = pl.BlockSpec((groups, width), source)
    return pl.pallas_call(
        up_dequant_kernel,
        grid_spec=pltpu.PrefetchScalarGridSpec(
            num_scalar_prefetch=1,
            grid=(2, RING),
            in_specs=[
                code_spec,
                group_spec,
                group_spec,
                code_spec,
                group_spec,
                group_spec,
                pl.BlockSpec((block, 128), source),
            ],
            out_specs=pl.BlockSpec(
                (2, 1, block // 2, 2 * width), lambda dc, d, place: (0, dc, d, 0)
            ),
        ),
        out_shape=pltpu.HBM((2, 2, model // 4, 2 * width), bf16),
        compiler_params=pltpu.CompilerParams(vmem_limit_bytes=20 * 1024 * 1024),
        cost_estimate=pl.CostEstimate(
            flops=8 * model * width, bytes_accessed=10 * model * width, transcendentals=0
        ),
        name="up_dequant",
    )(place, pinned(codes_a), zero_a, scale_a, pinned(codes_b), zero_b, scale_b, gain)


def down_dequant_kernel(place, codes, zero, scale, out):
    groups = zero.shape[0]
    size = codes.shape[0] // groups
    half = codes.shape[1] // 2
    for g in range(groups):
        rows = pl.ds(g * size, size)
        for part in range(2):
            cols = pl.ds(part * half, half)
            values = codes[rows, cols].astype(f32) - zero[pl.ds(g, 1), cols].astype(f32)
            out[0, part, rows, :] = (values * scale[pl.ds(g, 1), cols]).astype(bf16)


def down_dequant(place, codes, zero, scale):
    rows, model = codes.shape
    block = model // 8
    groups = zero.shape[0]

    def source(dc, d, place):
        return (0, d * 2 + lax.rem(place[1] + dc, 2))

    return pl.pallas_call(
        down_dequant_kernel,
        grid_spec=pltpu.PrefetchScalarGridSpec(
            num_scalar_prefetch=1,
            grid=(2, RING),
            in_specs=[
                pl.BlockSpec((rows, block), source),
                pl.BlockSpec((groups, block), source),
                pl.BlockSpec((groups, block), source),
            ],
            out_specs=pl.BlockSpec(
                (1, 2, rows, block // 2), lambda dc, d, place: (dc, 0, 0, d)
            ),
        ),
        out_shape=jax.ShapeDtypeStruct((2, 2, rows, model // 4), bf16),
        compiler_params=pltpu.CompilerParams(vmem_limit_bytes=20 * 1024 * 1024),
        cost_estimate=pl.CostEstimate(
            flops=3 * model * rows, bytes_accessed=4 * model * rows, transcendentals=0
        ),
        name="down_dequant",
    )(place, pinned(codes), zero, scale)


def pre_kernel(*refs, counts, last, model):
    sources, rest = refs[: sum(counts)], refs[sum(counts) :]
    w = rest[0]
    if last:
        pre_in, sq_in, out, rows, acc, sq, full, full_sq = rest[1:]
    else:
        out, sq_out, rows, acc, sq = rest[1:]
    part, k = pl.program_id(0), pl.program_id(1)
    steps = pl.num_programs(1)
    block = w.shape[2]
    width = w.shape[3]
    group = (pre_in if last else out).shape[0] // RING
    groups = rows.shape[0] // group
    per_side = counts[0] // 2

    for p in range(2):
        for side in range(2):
            first = p * counts[0] + side * per_side
            mine = sources[first : first + per_side]
            cols = pl.ds(side * block, block)
            @pl.when(part == p)
            def _(mine=mine, cols=cols):
                size = mine[0].shape[0]
                for g, source in enumerate(mine):
                    rows[pl.ds(g * size, size), cols] = source[...]

    product = jnp.dot(
        rows[...], w[0].reshape(2 * block, width), preferred_element_type=f32
    )

    def squares(at):
        total = None
        for j in range(2 * block // 128):
            v = rows[at, pl.ds(j * 128, 128)].astype(f32)
            total = v * v if total is None else total + v * v
        return total

    @pl.when(k == 0)
    def _():
        acc[part] = product
        for g in range(groups):
            at = pl.ds(g * group, group)
            sq[part, at, :] = squares(at)

    @pl.when(k > 0)
    def _():
        acc[part] += product
        for g in range(groups):
            at = pl.ds(g * group, group)
            sq[part, at, :] += squares(at)

    piece = group // RING

    @pl.when((part == 1) & (k == steps - 1))
    def _():
        if last:
            full[...] = pre_in[...]
            full_sq[...] = sq_in[...]
            for i in range(RING):
                down = pl.ds((i * RING + 2) * piece, piece)
                along = pl.ds((2 * RING + i) * piece, piece)
                here = pl.ds(i * piece, piece)
                full[down, :] += acc[0, here, :]
                full_sq[down, :] += sq[0, here, :]
                full[along, :] += acc[1, here, :]
                full_sq[along, :] += sq[1, here, :]
            half = width // 2
            for r in range(RING):
                at = pl.ds(r * group, group)
                square = jnp.sum(full_sq[at, :], axis=1, keepdims=True)
                scale = lax.rsqrt(square / model + epsilon)
                gate = full[at, :half] * scale
                up = full[at, half:] * scale
                out[at, :] = (jax.nn.silu(gate) * up).astype(bf16)
        else:
            place = {0: 0, 1: 1, 3: 2}
            for i in range(RING):
                for j in range(RING):
                    there = pl.ds((i * RING + j) * piece, piece)
                    total, total_sq = None, None
                    for p, major, minor in ((0, j, i), (1, i, j)):
                        if major == 2:
                            continue
                        here = pl.ds(place[major] * group + minor * piece, piece)
                        term, term_sq = acc[p, here, :], sq[p, here, :]
                        total = term if total is None else total + term
                        total_sq = term_sq if total_sq is None else total_sq + term_sq
                    if total is None:
                        total = jnp.zeros((piece, width), f32)
                        total_sq = jnp.zeros((piece, 128), f32)
                    out[there, :] = total
                    sq_out[there, :] = total_sq


def pre_product(parts, w_up, carried, model):
    last = carried is not None
    block_rows = parts[0][0][0].shape[0]
    group = block_rows * 2 if last else block_rows
    width = w_up.shape[-1]
    depth = w_up.shape[2]
    block = 1024
    steps = depth // block
    counts = tuple(len(own) + len(other) for own, other in parts)
    in_specs, operands = [], []
    for p, sides in enumerate(parts):
        for side in sides:
            for array in side:

                def index(part, k, p=p):
                    return (0, jnp.where(part == p, k, 0 if p else steps - 1))

                in_specs.append(pl.BlockSpec((block_rows, block), index))
                operands.append(array)
    in_specs.append(pl.BlockSpec((1, 2, block, width), lambda part, k: (part, 0, k, 0)))
    operands.append(w_up)
    total = RING * group
    rows = group if last else 3 * group

    def whole(*shape):
        return pl.BlockSpec(shape, lambda part, k: (0, 0))

    scratch = [
        pltpu.VMEM((rows, 2 * block), bf16),
        pltpu.VMEM((2, rows, width), f32),
        pltpu.VMEM((2, rows, 128), f32),
    ]
    if last:
        in_specs += [whole(total, width), whole(total, 128)]
        operands += list(carried)
        out_shape = jax.ShapeDtypeStruct((total, width // 2), bf16)
        out_specs = whole(total, width // 2)
        scratch += [pltpu.VMEM((total, width), f32), pltpu.VMEM((total, 128), f32)]
    else:
        out_shape = (
            jax.ShapeDtypeStruct((total, width), f32),
            jax.ShapeDtypeStruct((total, 128), f32),
        )
        out_specs = (whole(total, width), whole(total, 128))

    def kernel(*refs):
        pre_kernel(*refs, counts=counts, last=last, model=model)

    return pl.pallas_call(
        kernel,
        grid=(2, steps),
        in_specs=in_specs,
        out_specs=out_specs,
        out_shape=out_shape,
        scratch_shapes=scratch,
        compiler_params=pltpu.CompilerParams(vmem_limit_bytes=30 * 1024 * 1024),
        cost_estimate=pl.CostEstimate(
            flops=8 * rows * depth * width,
            bytes_accessed=8 * depth * (width + rows),
            transcendentals=0,
        ),
        name="pre_last" if last else "pre_first",
    )(*operands)


def column_sums(parts):
    row = lax.broadcasted_iota(jnp.int32, parts[0].shape, 0)
    shift = 1
    while len(parts) > 1:
        keep = (row // shift) % 2 == 0
        parts = [
            jnp.where(keep, a, b) + pltpu.roll(jnp.where(keep, b, a), shift, 0)
            for a, b in zip(parts[::2], parts[1::2])
        ]
        shift *= 2
    return parts[0]


def scan_kernel(own, got1, got2, got3, u, zin, dt_gain, dt_weight, dt_bias, a_log, skip,
                ssm, y_out, final, step, driven, bc, b_rows, c_rows, scanned):
    seq, low_rank = u.shape[0], dt_weight.shape[0]
    states, chans = a_log.shape

    def projected(cols):
        return (
            own[:, cols]
            + got1[:, cols].astype(f32)
            + got2[:, cols].astype(f32)
            + got3[:, cols].astype(f32)
        )

    low = projected(slice(0, low_rank))
    norm = low * lax.rsqrt(jnp.mean(low * low, axis=1, keepdims=True) + epsilon)
    norm = (norm * dt_gain[...]).astype(bf16)
    bc[...] = jnp.zeros_like(bc)
    bc[:, pl.ds(0, 2 * states)] = projected(slice(low_rank, low_rank + 2 * states))
    turned = bc[...].T
    for t in range(seq):
        b_rows[pl.ds(t * states, states), :] = jnp.broadcast_to(
            turned[:states, t : t + 1], (states, 128)
        )
        c_rows[pl.ds(t * states, states), :] = jnp.broadcast_to(
            turned[states : 2 * states, t : t + 1], (states, 128)
        )
    tile = 256
    for n in range(chans // tile):
        cols = pl.ds(n * tile, tile)
        raw = jnp.dot(norm, dt_weight[:, cols], preferred_element_type=f32) + dt_bias[:, cols]
        size = jnp.maximum(raw, 0.0) + jnp.log1p(jnp.exp(-jnp.abs(raw)))
        step[:, cols] = size
        driven[:, cols] = size * u[:, cols].astype(f32)
    log2e = 1.4426950408889634
    halves = states // 8
    tiles = chans // 128
    wide = 4
    unroll = 8
    for first in range(0, tiles, wide):
        span = range(first, first + wide)
        rate = [
            [jnp.exp(a_log[pl.ds(h * 8, 8), pl.ds(j * 128, 128)]) * (-log2e) for h in range(halves)]
            for j in span
        ]
        start = tuple(
            ssm[pl.ds(h * 8, 8), pl.ds(j * 128, 128)] for j in span for h in range(halves)
        )

        def advance(block, carried, span=span, rate=rate):
            carried = list(carried)
            at_rows = pl.ds(pl.multiple_of(block * unroll, unroll), unroll)
            base = block * (unroll * states)
            parts = [[] for _ in span]
            d_rows = [step[at_rows, pl.ds(j * 128, 128)] for j in span]
            du_rows = [driven[at_rows, pl.ds(j * 128, 128)] for j in span]
            for i in range(unroll):
                at_t = [
                    pl.ds(pl.multiple_of(base + i * states + h * 8, 8), 8) for h in range(halves)
                ]
                b_t = [b_rows[at, :] for at in at_t]
                c_t = [c_rows[at, :] for at in at_t]
                for n in range(len(span)):
                    d = d_rows[n][i : i + 1]
                    du = du_rows[n][i : i + 1]
                    out = None
                    for h in range(halves):
                        at = n * halves + h
                        carried[at] = jnp.exp2(d * rate[n][h]) * carried[at] + b_t[h] * du
                        term = c_t[h] * carried[at]
                        out = term if out is None else out + term
                    parts[n].append(out)
            for n, j in enumerate(span):
                scanned[at_rows, pl.ds(j * 128, 128)] = column_sums(parts[n])
            return tuple(carried)

        end = lax.fori_loop(0, seq // unroll, advance, start)
        for n, j in enumerate(span):
            for h in range(halves):
                final[pl.ds(h * 8, 8), pl.ds(j * 128, 128)] = end[n * halves + h]
    for n in range(chans // tile):
        cols = pl.ds(n * tile, tile)
        gate = zin[:, 1, :, cols].astype(f32).reshape(seq, tile)
        y = (scanned[:, cols] + skip[:, cols] * u[:, cols].astype(f32)) * jax.nn.silu(gate)
        y_out[:, cols] = y.astype(bf16)


def scan_mixer(own, got, u, zin, dt_gain, dt_weight, dt_bias, a_log, skip, ssm):
    seq, chans = u.shape
    states = a_log.shape[0]
    vmem = pl.BlockSpec(memory_space=pltpu.VMEM)
    return pl.pallas_call(
        scan_kernel,
        in_specs=[vmem] * 12,
        out_specs=(vmem, vmem),
        out_shape=(
            jax.ShapeDtypeStruct((seq, chans), bf16),
            jax.ShapeDtypeStruct((states, chans), f32),
        ),
        scratch_shapes=[
            pltpu.VMEM((seq, chans), f32),
            pltpu.VMEM((seq, chans), f32),
            pltpu.VMEM((seq, 128), f32),
            pltpu.VMEM((seq * states, 128), f32),
            pltpu.VMEM((seq * states, 128), f32),
            pltpu.VMEM((seq, chans), f32),
        ],
        compiler_params=pltpu.CompilerParams(vmem_limit_bytes=20 * 1024 * 1024),
        cost_estimate=pl.CostEstimate(
            flops=8 * seq * states * chans,
            bytes_accessed=16 * seq * chans,
            transcendentals=seq * states * chans,
        ),
        name="scan_mixer",
    )(own, *got, u, zin, dt_gain, dt_weight, dt_bias, a_log, skip, ssm)


def ranks(member):
    tokens = member.shape[-1]
    before = jnp.arange(tokens)[:, None] < jnp.arange(tokens)[None, :]
    return jnp.sum(
        jnp.where(before, member[..., :, None], 0), axis=-2
    )


def conv_project(x_shard, conv_state, conv_weight, conv_bias, proj_x):
    seq_len = x_shard.shape[0]
    kernel = conv_weight.shape[0]
    extended = jnp.concatenate([conv_state[0], x_shard], axis=0).astype(f32)
    conv_pre = jnp.broadcast_to(conv_bias.astype(f32), x_shard.shape)
    for shift_pos in range(kernel):
        conv_pre = conv_pre + extended[shift_pos : shift_pos + seq_len] * conv_weight[
            shift_pos
        ].astype(f32)
    u_act = jax.nn.silu(conv_pre).astype(bf16)
    return u_act, jnp.dot(u_act, proj_x, preferred_element_type=f32)


def body(
    x_in,
    z_in,
    conv_state,
    ssm_state,
    conv_weight,
    conv_bias,
    proj_x,
    dt_gain,
    dt_weight,
    dt_bias,
    a_log,
    skip_scale,
    out_weight,
    hidden,
    moe_gain,
    router,
    routes,
    gate_codes,
    gate_zero,
    gate_scale,
    up_codes,
    up_zero,
    up_scale,
    down_codes,
    down_zero,
    down_scale,
):
    z, core = lax.axis_index("z"), lax.axis_index("core")
    tok = x_in.shape[0]
    model = hidden.shape[1]
    experts = router.shape[1]
    cap = min(tok, (2 * tok + experts - 1) // experts + tok // 8)
    cols = model // 8
    half = cols // 2
    inner_cols = x_in.shape[1] // 16

    both = jnp.stack([x_in.reshape(tok, 16, inner_cols), z_in.reshape(tok, 16, inner_cols)])
    both, hidden = together(both.transpose(2, 0, 1, 3), hidden)
    both = lax.all_to_all(both, ("x", "y"), split_axis=0, concat_axis=0, tiled=True)
    hid = hidden.reshape(tok, RING, 2, cols)
    flags = jnp.pad(routes.astype(bf16), ((0, 0), (0, 126)))
    mine = jnp.concatenate([pick(hid, core, 2).reshape(tok, -1), flags], axis=1)
    theirs = jnp.concatenate([pick(hid, 1 - core, 2).reshape(tok, -1), flags], axis=1)
    pair = jnp.stack([mine, hop(theirs, "core", 1)])
    pair_cols = pair[..., : RING * cols].reshape(2, tok, RING, cols)
    pair_flags = pair[..., RING * cols :]
    pieces = [
        jnp.concatenate([pick(pair_cols, (z + d) % RING, 2), pair_flags], axis=-1)
        for d in range(RING)
    ]
    pieces = jnp.stack([pieces[0]] + [hop(pieces[d], "z", d) for d in (1, 2, 3)])
    conv_state, pieces = together(conv_state, pieces)
    hid_t = pieces[..., :cols].reshape(8 * tok, cols)
    route_t = pieces[..., cols : cols + 2].astype(jnp.int32)

    x_shard = both[:, 0].reshape(16 * tok, inner_cols)

    u_act, partial = conv_project(x_shard, conv_state, conv_weight, conv_bias, proj_x)
    sent = partial.astype(bf16)
    got = [hop(sent, "y", s) for s in (1, 2, 3)]
    partial = partial + sum(g.astype(f32) for g in got)
    sent = partial.astype(bf16)
    got = [hop(sent, "x", s) for s in (1, 2, 3)]

    d_ids = jnp.arange(RING)
    k_ids = (z + d_ids) % RING
    src_z = (z - d_ids) % RING
    src_core = (core + jnp.arange(2)) % 2
    src_e = src_z[:, None] * 2 + src_core[None, :]
    member = jnp.any(
        route_t[None] == k_ids[:, None, None, None, None], axis=-1
    ).astype(jnp.int32)
    slot = src_e[None, :, :, None] * cap + ranks(member)
    slot = jnp.where(member > 0, slot, -1)
    own = jnp.where(
        src_z[None, :, None, None] == k_ids[:, None, None, None],
        8 * cap + src_core[None, None, :, None] * tok + jnp.arange(tok)[None, None, None, :],
        -1,
    )
    slot, own = slot.reshape(RING, 1, 8 * tok), own.reshape(RING, 1, 8 * tok)
    row_ids = jnp.arange(8 * cap + 2 * tok)[None, :, None]
    select = ((slot == row_ids) | (own == row_ids)).astype(bf16)

    y_out, final_state = scan_mixer(
        partial,
        got,
        u_act,
        both,
        dt_gain.astype(f32)[None],
        dt_weight,
        dt_bias[None],
        a_log,
        skip_scale[None],
        ssm_state[0],
    )

    behind, ahead = hop(y_out, "z", 1), hop(y_out, "z", -1)
    split = y_out.shape[0] // 2
    far = together(behind[:split], ahead[split:])
    far = jnp.concatenate([hop(far[0], "z", 1), hop(far[1], "z", -1)], axis=0)
    blocks = [y_out, behind, far, ahead]
    blocks = [side for b in blocks for side in (b, hop(b, "core", 1))]
    y_all = jnp.concatenate([b.reshape(16, 1, tok, inner_cols) for b in blocks], axis=1)
    mixed = jnp.dot(
        y_all.reshape(-1, inner_cols), out_weight, preferred_element_type=f32
    ).astype(bf16)

    place = jnp.stack([z, core]).astype(jnp.int32)
    place, mixed = together(place, mixed)
    gain = jnp.broadcast_to(moe_gain.astype(f32)[:, None], (model, 128))
    w_up = up_dequant(
        place,
        gate_codes[0],
        gate_zero[0],
        gate_scale[0].astype(f32),
        up_codes[0],
        up_zero[0],
        up_scale[0].astype(f32),
        gain,
    )
    w_down = down_dequant(place, down_codes[0], down_zero[0], down_scale[0].astype(f32))

    mixed = lax.all_to_all(
        mixed.reshape(16, 8 * tok, cols), ("x", "y"), split_axis=0, concat_axis=0, tiled=True
    )
    mixed, w_up, w_down = together(mixed, w_up, w_down)

    rows = (hid_t.astype(f32) + jnp.sum(mixed.astype(f32), axis=0)).astype(bf16)
    rows = jnp.dot(select.reshape(-1, 8 * tok), rows, preferred_element_type=f32)
    rows = rows.astype(bf16).reshape(RING, -1, cols)
    arrived = [rows[0]] + [hop(rows[d], "z", d) for d in (1, 2, 3)]
    kept = jnp.stack([a[8 * cap :] for a in arrived]).reshape(RING, 2, tok, cols)

    def routed(part):
        return jnp.concatenate(
            [a[: 8 * cap, part * half : (part + 1) * half] for a in arrived], axis=1
        )

    def near(block, axis):
        return jnp.concatenate([block] + [hop(block, axis, d) for d in (1, 2, 3)], axis=0)

    routed_0, routed_1 = together(routed(0), routed(1))
    nears = together(near(routed_0, "x"), near(routed_1, "y"))
    axes = ("y", "x")
    behind = [hop(n, axis, 1) for n, axis in zip(nears, axes)]
    ahead = [hop(n, axis, -1) for n, axis in zip(nears, axes)]
    split = nears[0].shape[0] // 2
    pairs = [together(b[:split], a[split:]) for b, a in zip(behind, ahead)]
    passed = [pair[i] for i in range(2) for pair in pairs]
    across = [hop(passed[p], axes[p], 1) for p in range(2)]
    across += [hop(passed[2 + p], axes[p], -1) for p in range(2)]
    close = [[nears[p], behind[p], ahead[p]] for p in range(2)]
    carried = pre_product(
        [(own, [hop(c, "core", 1) for c in own]) for own in close], pinned(w_up), None, model
    )
    *across, pre_part, square_part = together(*across, *carried)
    last = [[across[p], across[2 + p]] for p in range(2)]
    inner_act = pre_product(
        [(own, [hop(c, "core", 1) for c in own]) for own in last],
        w_up,
        (pre_part, square_part),
        model,
    )
    units = inner_act.shape[-1]
    inner_act = inner_act.reshape(RING, RING, 8 * cap, units)

    def output(part, s):
        rows = lax.index_in_dim(inner_act, s, 1 if part == 0 else 0, keepdims=False)
        rows = rows.reshape(-1, units)
        away = jnp.dot(rows, w_down[1, part], preferred_element_type=f32).astype(bf16)
        here = jnp.dot(rows, w_down[0, part], preferred_element_type=f32)
        return here + hop(away, "core", 1).astype(f32)

    total_0, total_1 = ring_sums(
        [output(part, 2).astype(bf16) for part in range(2)],
        lambda: [[output(part, s) for s in (0, 1, 3)] for part in range(2)],
        ("y", "x"),
        -1,
    )
    total_0 = total_0.reshape(RING, 8 * cap, -1)
    total_1 = total_1.reshape(RING, 8 * cap, -1)
    terms = [
        total[s].astype(bf16 if s else f32) for total in (total_0, total_1) for s in range(RING)
    ]
    total_0 = gather_sum(terms[:RING], "x", -1).astype(bf16)
    total_1 = gather_sum(terms[RING:], "y", -1).astype(bf16)
    sums = jnp.concatenate([total_0, total_1], axis=1).reshape(RING, 2 * cap, -1)
    back = [pick(sums, (z + d) % RING, 0) for d in range(RING)]
    back = jnp.stack([back[0]] + [hop(back[d], "z", d) for d in (1, 2, 3)])
    back = back.reshape(RING, 2, cap, -1)
    back_own = pick(back, core, 1).reshape(RING * cap, -1)
    back_other = hop(pick(back, 1 - core, 1), "core", 1).reshape(RING * cap, -1)

    res_own = pick(kept, core, 1)
    res_other = hop(pick(kept, 1 - core, 1), "core", 1)

    def ordered(own_part, other_part):
        low = jnp.where(core == 0, own_part, other_part)
        high = jnp.where(core == 0, other_part, own_part)
        return jnp.stack([low, high], axis=1).transpose(2, 0, 1, 3).reshape(tok, model)

    def absolute(value):
        return jnp.stack([pick(value, (z - i) % RING, 0) for i in range(RING)])

    residual = ordered(absolute(res_own), absolute(res_other)).astype(f32)
    normed = (
        residual
        * lax.rsqrt(jnp.mean(residual * residual, axis=1, keepdims=True) + epsilon)
        * moe_gain.astype(f32)
    ).astype(bf16)
    logits = jnp.dot(normed, router, preferred_element_type=f32)
    weights = jnp.exp(logits)
    probs = weights / jnp.sum(weights, axis=1, keepdims=True)
    named = jnp.any(routes[None] == jnp.arange(experts)[:, None, None], axis=-1)
    rank = ranks(named.astype(jnp.int32))
    gates = jnp.where(
        named[:, :, None] & (rank[:, :, None] == jnp.arange(cap)), probs.T[:, :, None], 0.0
    )
    gates = jnp.stack([pick(gates, (z - d) % RING, 0) for d in range(RING)])
    gates = gates.transpose(1, 0, 2).reshape(tok, RING * cap)

    def combined(rows):
        out = jnp.dot(gates, rows.astype(f32), precision=lax.Precision.HIGHEST)
        return out.reshape(tok, 2, RING, half).transpose(2, 0, 1, 3).reshape(RING, tok, cols)

    layer_out = (residual + ordered(combined(back_own), combined(back_other))).astype(bf16)
    return (layer_out, final_state[None])


def solution(mesh):
    fine = Mesh(mesh.devices.reshape(RING, 2, RING, RING), ("z", "core", "x", "y"))
    e, c = ("z", "core"), ("x", "y")
    every = e + c
    return jax.shard_map(
        body,
        mesh=fine,
        in_specs=(
            P(every, None),
            P(every, None),
            P(e, None, c),
            P(e, None, c),
            P(None, c),
            P(c),
            P(c, None),
            P(),
            P(None, c),
            P(c),
            P(None, c),
            P(c),
            P(c, e),
            P(every, None),
            P(),
            P(),
            P(every, None),
            P(e, None, c),
            P(e, None, c),
            P(e, None, c),
            P(e, None, c),
            P(e, None, c),
            P(e, None, c),
            P(e, c, None),
            P(e, c, None),
            P(e, c, None),
        ),
        out_specs=(P(every, None), P(e, None, c)),
        check_vma=False,
    )
```
